256 devices in a mesh: atoms: 32 (over x, y, core), kvec: 8 (over z).
Axes of the slice: x: 4, y: 4, z: 8, core: 2. Of those that a mesh axis runs over, the one named last changes fastest.
Arguments:
- positions: float32 [3, 131072], P(None, 'atoms'), may hold values from 0 to 1
- features: bfloat16 [131072, 128], P('atoms'), may hold values from -6 to 6
- charge_weight: bfloat16 [128, 32], replicated, may hold values from -0.5 to 0.5
- counts: int32 [32], P('atoms'), may hold values from 1 to 4096, 81920 in all
- mol_ids: int32 [32, 4096], P('atoms'), may hold values from 0 to 255, never falling along the last dimension, each value on 1 to 32 neighbouring positions
- energy_cot: float32 [8192], P('atoms'), may hold values from -6 to 6
- lattice: int32 [3, 8192], P(None, 'kvec'), may hold values from -12 to 12, as said below
- filter_in: bfloat16 [16, 256], replicated, may hold values from -1.5 to 1.5
- filter_mid: bfloat16 [256, 256], replicated, may hold values from -0.375 to 0.375
- filter_out: bfloat16 [256, 32], replicated, may hold values from -0.375 to 0.375
Outputs:
- mol_energy: float32 [8192], P('atoms')
- position_grad: float32 [3, 131072], P(None, ('atoms', 'kvec'))
- charge_grad: float32 [128, 32], replicated
- filter_in_grad: float32 [16, 256], replicated
- filter_mid_grad: float32 [256, 256], replicated
- filter_out_grad: float32 [256, 32], replicated
The draws below stay inside these ranges and needn't reach their ends.
Inputs may be any that keep to these rules, and one draw needn't show every extreme that they name: `counts`: each group's count is at least 1 and at most 4096; some group holds exactly 4096 live atoms. `mol_ids`: within a group, ids never fall along the slots; each molecule has 1 to 32 slots; ids of dead slots are ignored. `lattice`: no k-vector has all three indices zero.
All inputs are finite; a program needn't handle non-finite values.
Results may differ from the reference program's by a relative error of at most 0.035.
Values may be sent and summed in bfloat16 or wider, within the bound.
A program may use at most 128 MiB of HBM per device.

```python
import math
import jax
import jax.numpy as jnp
import numpy as np
from jax import lax

F = 128
C = 32
H = 256
NB = 16
MAXN = 12
CAP = 4096
MOL_DEV = 256
SHARDS = 32
ATOMS = 131072
MOLS = 8192
K = 8192


def draw_lattice(key, part):
    key = jax.random.fold_in(key, 7)
    indices = jax.random.randint(key, (3, K), -MAXN, MAXN + 1, dtype=jnp.int32)
    nought = jnp.all(indices == 0, axis=0)
    indices = indices.at[0].set(jnp.where(nought, 1, indices[0]))
    indices = indices.at[0, 0].set(MAXN)
    indices = indices.at[0, 1].set(-MAXN)
    return indices.astype(jnp.int32)


def levels(key, shape, shards, smallest, high):
    level, own = 1.0, jax.random.fold_in(key, 6)
    for position, blocks in shards:
        steps = jnp.exp(jax.random.uniform(jax.random.fold_in(own, position), (blocks,), jnp.float32, smallest / len(shards), high / len(shards)))
        level = level * jnp.repeat(steps, shape[position] // blocks).reshape([-1 if axis == position else 1 for axis in range(len(shape))])
    return level


def split_up(amount, total, reach, skew):
    loads = [(1 << 20) // math.isqrt(rank ** skew) + 1 for rank in range(2, amount + 1)]
    surplus, given = total - reach - (amount - 1), [1] * (amount - 1)
    while surplus > 0:
        free = [i for i in range(amount - 1) if given[i] < reach]
        mass, left = sum([loads[i] for i in free]), surplus
        for i in free:
            addition = min(reach - given[i], max(1, left * loads[i] // mass), surplus)
            given[i] = given[i] + addition
            surplus = surplus - addition
    return np.array([reach] + given)


def ragged_sizes(rng, count, total, bound, lean):
    if count == 2:
        one = jax.random.randint(rng, (), max(1, total - bound), min(bound, total - 1) + 1)
        return jnp.stack([one, total - one])
    tallies = jnp.asarray(split_up(count, total, bound, lean), jnp.int32)
    pairs = (count - 1) // 2
    donor, receiver = tallies[1:1 + 2 * pairs:2], tallies[2:2 + 2 * pairs:2]
    slack = jnp.minimum(donor - 1, bound - receiver)
    moved = jax.random.randint(jax.random.fold_in(rng, 1), (pairs,), 0, 1 << 20) % (slack + 1)
    tallies = tallies.at[1:1 + 2 * pairs:2].set(donor - moved).at[2:2 + 2 * pairs:2].set(receiver + moved)
    return tallies[jax.random.permutation(jax.random.fold_in(rng, 2), count)]


def noise(rng, shape, deviation, reach, shards=(), kind=jnp.bfloat16):
    result = deviation * jax.random.normal(rng, shape, jnp.float32)
    if shards:
        result = result * levels(rng, shape, shards, -0.22, 0.18)
    return jnp.clip(result, -reach, reach).astype(kind)


def setup_inputs(seed: int = 0) -> dict:
    arg_keys = jax.random.split(jax.random.key(seed), 11)
    positions = jnp.clip(1.0 * jax.random.uniform(arg_keys[0], (3, ATOMS), jnp.float32) ** levels(arg_keys[0], (3, ATOMS), ((1, 32),), -0.2, 0.2), 0.0, 1.0)
    features = noise(arg_keys[1], (ATOMS, F), 1.0, 6.0, ((0, 32),))
    charge_weight = noise(arg_keys[2], (F, C), F ** -0.5, 0.5)
    counts = ragged_sizes(arg_keys[3], SHARDS, (SHARDS * CAP * 5) // 8, CAP, 2).astype(jnp.int32)
    mol_ids = jax.vmap(lambda own: jnp.searchsorted(jnp.cumsum(ragged_sizes(own, MOL_DEV, CAP, 32, 1)), jnp.arange(CAP), side="right"))(jax.random.split(arg_keys[4], SHARDS)).reshape((SHARDS, CAP)).astype(jnp.int32)
    energy_cot = noise(arg_keys[5], (MOLS,), 1.0, 6.0, ((0, 32),), jnp.float32)
    lattice = draw_lattice(jax.random.fold_in(arg_keys[10], 71), 0)
    filter_in = noise(arg_keys[7], (NB, H), NB ** -0.5, 1.5)
    filter_mid = noise(arg_keys[8], (H, H), H ** -0.5, 0.375)
    filter_out = noise(arg_keys[9], (H, C), H ** -0.5, 0.375)
    return {"positions": positions, "features": features, "charge_weight": charge_weight, "counts": counts, "mol_ids": mol_ids, "energy_cot": energy_cot, "lattice": lattice, "filter_in": filter_in, "filter_mid": filter_mid, "filter_out": filter_out}


BOX_EDGE = 40.0

def contract_first(first_op, second_op):
    return lax.dot_general(first_op, second_op, (((0,), (0,)), ((), ())), preferred_element_type=jnp.float32)

def contract_last(first_op, second_op):
    return lax.dot_general(first_op, second_op, (((1,), (1,)), ((), ())), preferred_element_type=jnp.float32)

def slope(preact):
    sigmoid_val = jax.nn.sigmoid(preact)
    return sigmoid_val * (1.0 + preact * (1.0 - sigmoid_val))

def filter_pass(lattice, filter_in, filter_mid, filter_out, spectrum, total_atoms):
    channels = filter_out.shape[1]
    lattice_f = lattice.astype(jnp.float32)
    squared = lax.optimization_barrier(jnp.sum(lattice_f * lattice_f, axis=0))
    inverse = 1.0 / (squared * math.sqrt(total_atoms))
    radius = jnp.sqrt(squared)
    num_basis = filter_in.shape[0]
    spacing = MAXN * math.sqrt(3.0) / num_basis
    centers = (jnp.arange(num_basis, dtype=jnp.float32) + 0.5) * spacing
    offset = (radius[None, :] - centers[:, None]) / spacing
    radial = jnp.exp(-0.5 * offset * offset).astype(jnp.bfloat16)
    pre_one = contract_first(filter_in, radial)
    act_one = jax.nn.silu(pre_one).astype(jnp.bfloat16)
    pre_two = contract_first(filter_mid, act_one)
    act_two = jax.nn.silu(pre_two).astype(jnp.bfloat16)
    logits = contract_first(filter_out, act_two)
    filters = (jax.nn.softplus(logits) * inverse[None, :]).T
    shaped = spectrum.reshape(spectrum.shape[0], 2, 2 * channels)
    spec_cos = shaped[:, 0, :channels]
    twin_cos = shaped[:, 0, channels:]
    spec_sin = shaped[:, 1, :channels]
    twin_sin = shaped[:, 1, channels:]
    coefficients = jnp.stack([jnp.concatenate([filters * spec_cos, filters * twin_cos], axis=1), jnp.concatenate([filters * spec_sin, filters * twin_sin], axis=1)], axis=1).astype(jnp.bfloat16)
    upstream = 0.5 * (spec_cos * twin_cos + spec_sin * twin_sin)
    grad_logits = (upstream.T * jax.nn.sigmoid(logits) * inverse[None, :]).astype(jnp.bfloat16)
    out_grad = contract_last(act_two, grad_logits)
    grad_two = (jnp.dot(filter_out, grad_logits, preferred_element_type=jnp.float32) * slope(pre_two)).astype(jnp.bfloat16)
    mid_grad = contract_last(act_one, grad_two)
    grad_one = (jnp.dot(filter_mid, grad_two, preferred_element_type=jnp.float32) * slope(pre_one)).astype(jnp.bfloat16)
    in_grad = contract_last(radial, grad_one)
    return (coefficients, in_grad, mid_grad, out_grad)

def reference(positions, features, charge_weight, counts, mol_ids, energy_cot, lattice, filter_in, filter_mid, filter_out):
    shard_count, capacity = mol_ids.shape
    total_atoms = shard_count * capacity
    channels = charge_weight.shape[1]
    kcount = lattice.shape[1]
    per_group = energy_cot.shape[0] // shard_count
    block_rows = max(min(512, capacity), capacity // 8)
    nblocks = total_atoms // block_rows
    slots = jnp.arange(capacity, dtype=jnp.int32)
    alive = (slots[None, :] < counts[:, None]).astype(jnp.float32).reshape(total_atoms)
    global_mol = (mol_ids + jnp.arange(shard_count, dtype=jnp.int32)[:, None] * per_group).reshape(total_atoms)
    weight_atom = energy_cot[global_mol]
    charge = (jnp.dot(features, charge_weight, preferred_element_type=jnp.float32) * alive[:, None]).astype(jnp.bfloat16)
    weighted = (weight_atom[:, None] * charge.astype(jnp.float32)).astype(jnp.bfloat16)
    paired = jnp.concatenate([charge, weighted], axis=1)
    swapped = jnp.concatenate([weighted, charge], axis=1)
    wavevec = 2.0 * math.pi * lattice.astype(jnp.float32)
    pos_blocks = positions.reshape(3, nblocks, block_rows).transpose(1, 0, 2)
    pair_blocks = paired.reshape(nblocks, block_rows, 2 * channels)
    swap_blocks = swapped.reshape(nblocks, block_rows, 2 * channels)

    def phases(coords):
        angles = jnp.dot(coords.T, wavevec, precision=lax.Precision.HIGHEST)
        return jnp.stack([jnp.cos(angles), jnp.sin(angles)]).astype(jnp.bfloat16)

    def accumulate(carried, bundle):
        coords, pair_rows = bundle
        phasors = phases(coords).astype(jnp.float32)
        term = jnp.einsum('sbk,bc->ksc', phasors, pair_rows.astype(jnp.float32), precision=lax.Precision.HIGHEST)
        return (carried + term, None)
    spectrum, _ = lax.scan(accumulate, jnp.zeros((kcount, 2, 2 * channels), jnp.float32), (pos_blocks, pair_blocks))
    coefficients, in_grad, mid_grad, out_grad = filter_pass(lattice, filter_in, filter_mid, filter_out, spectrum.reshape(kcount, 4 * channels), total_atoms)
    coef_f = coefficients.astype(jnp.float32)

    def second(bundle):
        coords, swap_rows = bundle
        phasors = phases(coords).astype(jnp.float32)
        potentials = jnp.einsum('sbk,ksc->bc', phasors, coef_f, precision=lax.Precision.HIGHEST)
        response = jnp.einsum('bc,ksc->sbk', swap_rows.astype(jnp.float32), coef_f, precision=lax.Precision.HIGHEST)
        angle_grad = 0.5 * (phasors[0] * response[1] - phasors[1] * response[0])
        pos_grad = jnp.dot(wavevec, angle_grad.T, precision=lax.Precision.HIGHEST) / BOX_EDGE
        return (potentials, pos_grad)
    potentials, pos_grad = lax.map(second, (pos_blocks, swap_blocks))
    potentials = potentials.reshape(total_atoms, 2 * channels)
    position_grad = pos_grad.transpose(1, 0, 2).reshape(3, total_atoms)
    volt = potentials[:, :channels]
    other = potentials[:, channels:]
    atom_energy = 0.5 * lax.optimization_barrier(jnp.sum(charge.astype(jnp.float32) * volt, axis=1))
    mol_energy = jax.ops.segment_sum(atom_energy, global_mol, num_segments=energy_cot.shape[0])
    charge_cot = (0.5 * (weight_atom[:, None] * volt + other) * alive[:, None]).astype(jnp.bfloat16)
    charge_grad = contract_first(features, charge_cot)
    return (mol_energy, position_grad, charge_grad, in_grad, mid_grad, out_grad)
```

```python
import functools
import math

import jax
import jax.numpy as jnp
import numpy as np
from jax import lax
from jax.experimental import pallas as pl
from jax.experimental.pallas import tpu as pltpu
from jax.sharding import PartitionSpec as P

MAXN = 12
BOX_EDGE = 40.0
MESH = pl.DeviceIdType.MESH
F32 = jnp.float32
BF16 = jnp.bfloat16

PLANE = 32
RING = 8
CAP = 4096
CH = 32
HID = 256
MOLS = 256
YZ = 640
XC = 256
HALF = 320
TILE = 512
TILES = CAP // TILE
CHIPS = 16
PAIR_ROWS = 80
BIG = 48
SMALL = 32
TABLE = 512
FAR_FIRST = (4, 3, 5, 2, 6, 1, 7)
MIB = 1 << 20


def row_of(y_index, z_index):
    if y_index is None and z_index is None:
        return 624
    if y_index is None:
        return 576 + z_index
    if z_index is None:
        return 600 + y_index
    return 24 * y_index + z_index


def half_plane():
    vectors = [(0, n3) for n3 in range(13)]
    return vectors + [(n2, n3) for n2 in range(1, 13) for n3 in range(-12, 13)]


def sign_matrix():
    def cosine(n):
        return None if n == 0 else n - 1

    def sine(n):
        return 12 + n - 1

    matrix = np.zeros((2 * HALF, YZ), np.float32)
    for index, (n2, n3) in enumerate(half_plane()):
        size, sign = abs(n3), (1.0 if n3 >= 0 else -1.0)
        matrix[index, row_of(cosine(n2), cosine(size))] = 1.0
        if n2 and size:
            matrix[index, row_of(sine(n2), sine(size))] = -sign
        if n2:
            matrix[HALF + index, row_of(sine(n2), cosine(size))] = 1.0
        if size:
            matrix[HALF + index, row_of(cosine(n2), sine(size))] = sign
    return matrix


def nt(first, second):
    return lax.dot_general(first, second, (((1,), (1,)), ((), ())), preferred_element_type=F32)


def tn(first, second):
    return lax.dot_general(first, second, (((0,), (0,)), ((), ())), preferred_element_type=F32)


def nn(first, second):
    return jnp.dot(first, second, preferred_element_type=F32)


def cos_turns(turns):
    frac = turns - jnp.floor(turns + 0.5)
    x = (2.0 * math.pi) * (0.25 - jnp.abs(frac))
    s = x * x
    poly = jnp.full_like(s, -1.0 / 39916800.0)
    for coefficient in (1.0 / 362880.0, -1.0 / 5040.0, 1.0 / 120.0, -1.0 / 6.0, 1.0):
        poly = poly * s + coefficient
    return x * poly


def rows_of_parts(value):
    high = value.astype(BF16).astype(F32)
    rest = value - high
    middle = rest.astype(BF16).astype(F32)
    low = rest - middle
    row = lax.broadcasted_iota(jnp.int32, (16, value.shape[1]), 0)
    parts = jnp.where(row == 0, high, jnp.where(row == 1, middle, jnp.where(row == 2, low, 0.0)))
    return parts.astype(BF16)


def yz_turns(coord):
    row = lax.broadcasted_iota(jnp.int32, (24, 1), 0)
    harmonic = jnp.where(row < 12, row + 1, row - 11).astype(F32)
    shift = jnp.where(row < 12, 0.0, 0.25)
    return harmonic * coord - shift, harmonic


def x_turns(coord, rank):
    row = lax.broadcasted_iota(jnp.int32, (8, 1), 0)
    harmonic = (2 * rank + lax.rem(row, 2)).astype(F32)
    shift = jnp.where(row < 2, 0.0, 0.25)
    return harmonic * coord - shift, harmonic


def lane_roll(value, shift):
    return pltpu.roll(value, shift % value.shape[1], 1)


def slope(preact, sigmoid_val):
    return sigmoid_val * (1.0 + preact * (1.0 - sigmoid_val))


def point_squares(rank, axis):
    dims = (2 * HALF, 1) if axis == 0 else (1, 2 * HALF)
    index = lax.broadcasted_iota(jnp.int32, dims, axis)
    n1 = (2 * rank + jnp.where(index >= HALF, 1, 0)).astype(F32)
    index = jnp.where(index >= HALF, index - HALF, index)
    later = (index - 13).astype(F32)
    n2 = jnp.where(index < 13, 0.0, 1.0 + jnp.floor((later + 0.5) * (1.0 / 25.0)))
    n3 = jnp.where(index < 13, index.astype(F32), later - 25.0 * (n2 - 1.0) - 12.0)
    return n1 * n1 + n2 * n2 + n3 * n3


def loop(low, high, action):
    def run(i, carry):
        action(i)
        return carry

    lax.fori_loop(low, high, run, 0)


def first_pass(rank, count, v, half):
    cot_parts = rows_of_parts(v.cot[...])
    for tile in range(half * TILES // 2, (half + 1) * TILES // 2):
        at = pl.ds(tile * TILE, TILE)
        slot = tile * TILE + lax.broadcasted_iota(jnp.int32, (1, TILE), 1)
        alive = jnp.where(slot < count, 1.0, 0.0)
        v.alive[:, at] = alive
        molecule = lax.broadcasted_iota(jnp.int32, (MOLS, TILE), 0)
        member = jnp.where(molecule == v.ids[:, at], 1.0, 0.0).astype(BF16)
        v.member[:, at] = member
        weight = jnp.sum(nn(cot_parts, member), axis=0, keepdims=True)
        v.weight[:, at] = weight
        charge = (nt(v.cw[...], v.feat[at, :]) * alive).astype(BF16).astype(F32)
        pair = jnp.concatenate([charge, weight * charge], axis=0).astype(BF16)
        v.pair[:, at] = pair
        pair = pair.astype(F32)
        turns2, _ = yz_turns(v.pos[1:2, at])
        turns3, _ = yz_turns(v.pos[2:3, at])
        turns1, _ = x_turns(v.pos[0:1, at], rank)
        v.u2[:, at] = cos_turns(turns2)
        v.u3[:, at] = cos_turns(turns3)
        v.u1[:, at] = cos_turns(turns1)
        u3 = v.u3[:, at]
        for two in range(12):
            first = v.u2[2 * two : 2 * two + 1, at] * u3
            second = v.u2[2 * two + 1 : 2 * two + 2, at] * u3
            rows = jnp.concatenate([first, second], axis=0).astype(BF16)
            v.b[48 * two : 48 * two + 48, at] = rows
        v.b[576:624, at] = jnp.concatenate([u3, v.u2[:, at]], axis=0).astype(BF16)
        row = lax.broadcasted_iota(jnp.int32, (16, TILE), 0)
        v.b[624:640, at] = jnp.where(row == 0, 1.0, 0.0).astype(BF16)
        for j in range(4):
            v.a[64 * j : 64 * j + 64, at] = (v.u1[j : j + 1, at] * pair).astype(BF16)


def structure_sum(v, half):
    at = pl.ds(half * CAP // 2, CAP // 2)
    return nt(v.b[:, at], v.a[:, at])


def network(squared, v):
    inverse = jnp.where(squared > 0.0, 1.0, 0.0) / (
        jnp.maximum(squared, 1.0) * math.sqrt(CAP * PLANE)
    )
    spacing = MAXN * math.sqrt(3.0) / 16
    center = (lax.broadcasted_iota(jnp.int32, (1, 16), 1).astype(F32) + 0.5) * spacing
    away = (jnp.sqrt(squared) - center) / spacing
    radial = jnp.exp(-0.5 * away * away).astype(BF16)
    pre_one = nn(radial, v.fin[...])
    sig_one = jax.nn.sigmoid(pre_one)
    act_one = (pre_one * sig_one).astype(BF16)
    pre_two = nn(act_one, v.fmid[...])
    sig_two = jax.nn.sigmoid(pre_two)
    act_two = (pre_two * sig_two).astype(BF16)
    logits = nn(act_two, v.fout_wide[...])
    return inverse, radial, pre_one, sig_one, act_one, pre_two, sig_two, act_two, logits


def filter_forward(rank, v):
    lane = lax.broadcasted_iota(jnp.int32, (CH, 128), 1)
    channel = lax.broadcasted_iota(jnp.int32, (CH, 128), 0)
    spread = jnp.where(lax.rem(lane, CH) == channel, 1.0, 0.0).astype(BF16)
    v.fout_wide[...] = tn(v.fout[...], spread).astype(BF16)
    values = network(point_squares(rank, 0), v)
    inverse, logits = values[0], values[-1]
    soft = jnp.maximum(logits, 0.0) + jnp.log1p(jnp.exp(-jnp.abs(logits)))
    soft = soft * inverse
    half_lane = lax.broadcasted_iota(jnp.int32, (HALF, 128), 1)
    v.filters[...] = jnp.where(half_lane < 64, soft[:HALF], soft[HALF:])


def table_forward(rank, v):
    table = lax.broadcasted_iota(jnp.int32, (TABLE, 1), 0).astype(F32)
    inverse, radial, pre_one, sig_one, act_one, pre_two, sig_two, act_two, logits = network(table, v)
    v.radial[...] = radial
    v.act_one[...] = act_one
    v.act_two[...] = act_two
    v.slope_one[...] = slope(pre_one, sig_one)
    v.slope_two[...] = slope(pre_two, sig_two)
    v.sigmoid[...] = jax.nn.sigmoid(logits) * inverse
    v.same[...] = jnp.where(table == point_squares(rank, 1), 1.0, 0.0).astype(BF16)


def multiplicities(rank, v):
    def chunk(index, total):
        k = v.lattice[index]
        k1, k2, k3 = k[0:1, :], k[1:2, :], k[2:3, :]
        back = k1 < 0
        k1 = jnp.where(back, -k1, k1)
        k2 = jnp.where(back, -k2, k2)
        k3 = jnp.where(back, -k3, k3)
        flip = (k2 < 0) | ((k2 == 0) & (k3 < 0))
        k2 = jnp.where(flip, -k2, k2)
        k3 = jnp.where(flip, -k3, k3)
        code = jnp.where(k2 == 0, k3, k2 * 25 + k3)
        width = k.shape[1]
        hit = lax.broadcasted_iota(jnp.int32, (HALF, width), 0) == code
        hit = jnp.where(hit, 1.0, 0.0).astype(BF16)
        row = lax.broadcasted_iota(jnp.int32, (16, width), 0)
        own = (k1 - 2 * rank) == lax.rem(row, 2)
        sign = jnp.where((row >= 2) & flip, -1.0, 1.0)
        select = jnp.where(own & (row < 4), sign, 0.0).astype(BF16)
        return total + nt(hit, select)

    counted = lax.fori_loop(0, RING, chunk, jnp.zeros((HALF, 16), F32))
    lane = lax.broadcasted_iota(jnp.int32, (HALF, 128), 1)
    v.both[...] = jnp.where(lane < 64, counted[:, 0:1], counted[:, 1:2])
    v.difference[...] = jnp.where(lane < 64, counted[:, 2:3], counted[:, 3:4])


def coefficients(v):
    signs = v.signs[...]
    total = jnp.concatenate([v.total[:YZ, :], v.total[YZ:, :]], axis=1)
    v.sums[...] = nn(signs, total)
    ncc, ncs = v.sums[:HALF, :128], v.sums[HALF:, :128]
    nsc, nss = v.sums[:HALF, 128:], v.sums[HALF:, 128:]
    filters = v.filters[...]
    fp, fd = filters * v.both[...], filters * v.difference[...]
    gcc = (fp * ncc - fd * nss).astype(BF16)
    gss = (fp * nss - fd * ncc).astype(BF16)
    gsc = (fp * nsc + fd * ncs).astype(BF16)
    gcs = (fp * ncs + fd * nsc).astype(BF16)
    v.coef[:HALF, :128] = gcc
    v.coef[HALF:, :128] = gcs
    v.coef[:HALF, 128:] = gsc
    v.coef[HALF:, 128:] = gss
    v.gt[...] = tn(v.coef[...], signs).astype(BF16)


def swapped_coefficients(v):
    g = nn(v.signs_t[...], v.coef[...])
    lane = lax.broadcasted_iota(jnp.int32, (YZ, XC), 1)
    swapped = jnp.where(lax.rem(lane, 64) < 32, lane_roll(g, -32), lane_roll(g, 32))
    v.gs[...] = swapped.astype(BF16)


def upstream_table(v):
    ncc, ncs = v.sums[:HALF, :128], v.sums[HALF:, :128]
    nsc, nss = v.sums[:HALF, 128:], v.sums[HALF:, 128:]
    tcc, tcs = lane_roll(ncc, -32), lane_roll(ncs, -32)
    tsc, tss = lane_roll(nsc, -32), lane_roll(nss, -32)
    upstream = 0.5 * (
        v.both[...] * (ncc * tcc + nss * tss + nsc * tsc + ncs * tcs)
        + v.difference[...] * (nsc * tcs + ncs * tsc - ncc * tss - nss * tcc)
    )
    upstream = jnp.concatenate([upstream, lane_roll(upstream, -64)], axis=0)
    lane = lax.broadcasted_iota(jnp.int32, (2 * HALF, 128), 1)
    upstream = jnp.where(lane < CH, upstream, 0.0)
    total = nn(v.same[0:128, :], upstream.astype(BF16))
    for group in range(1, 4):
        rows = v.same[128 * group : 128 * group + 128, :]
        total = total + nn(rows, lane_roll(upstream, 32 * group).astype(BF16))
    return total.astype(BF16)


def filter_backward(v):
    upstream = v.up_total[...].astype(F32)
    upstream = jnp.concatenate(
        [upstream] + [lane_roll(upstream, -32 * group) for group in range(1, 4)], axis=0
    )
    lane = lax.broadcasted_iota(jnp.int32, (TABLE, 128), 1)
    grad_logits = jnp.where(lane < CH, upstream * v.sigmoid[...], 0.0).astype(BF16)
    out_grad = tn(grad_logits, v.act_two[...])
    grad_two = (nt(grad_logits, v.fout_wide[...]) * v.slope_two[...]).astype(BF16)
    v.mid_grad[...] = tn(v.act_one[...], grad_two)
    grad_one = (nt(grad_two, v.fmid[...]) * v.slope_one[...]).astype(BF16)
    v.in_grad[...] = tn(v.radial[...], grad_one)
    v.out_grad[...] = out_grad[:CH]


GRAD_SCALE = 0.5 * 2.0 * math.pi / BOX_EDGE


def potential_pass(rank, v):
    for tile in range(TILES):
        at = pl.ds(tile * TILE, TILE)
        turns1, h1 = x_turns(v.pos[0:1, at], rank)
        d1 = h1 * cos_turns(turns1 + 0.25)
        u1 = v.u1[:, at]
        pair = v.pair[:, at].astype(F32)
        charge, weighted = pair[:CH], pair[CH:]
        w = nn(v.gt[...], v.b[:, at])
        pot = sum(u1[j : j + 1, :] * w[64 * j : 64 * j + 64, :] for j in range(4))
        potx = sum(d1[j : j + 1, :] * w[64 * j : 64 * j + 64, :] for j in range(4))
        volt, other = pot[:CH], pot[CH:]
        grad_x = jnp.sum(weighted * potx[:CH] + charge * potx[CH:], axis=0, keepdims=True)
        v.message[tile, 0:1, :] = grad_x * GRAD_SCALE
        v.energy[:, at] = 0.5 * jnp.sum(charge * volt, axis=0, keepdims=True)
        v.cot_rows[:, at] = (0.5 * (v.weight[:, at] * volt + other) * v.alive[:, at]).astype(BF16)
    return nn(v.cot_rows[...], v.feat[...])


def molecule_sums(v):
    return jnp.sum(nt(rows_of_parts(v.energy[...]), v.member[...]), axis=0, keepdims=True)


def force_pass(v):
    def fold(value):
        return value[0:8] + value[8:16] + value[16:24]

    for tile in range(TILES):
        at = pl.ds(tile * TILE, TILE)
        turns2, h2 = yz_turns(v.pos[1:2, at])
        turns3, h3 = yz_turns(v.pos[2:3, at])
        v.d2[:, at] = h2 * cos_turns(turns2 + 0.25)
        v.response[:, at] = nn(v.gs[...], v.a[:, at])
        u3, d3 = v.u3[:, at], h3 * cos_turns(turns3 + 0.25)
        sum_y = fold(v.d2[:, at] * v.response[600:624, at])
        sum_z = fold(d3 * v.response[576:600, at])
        for y in range(24):
            response = v.response[24 * y : 24 * y + 24, at]
            sum_y = sum_y + v.d2[y : y + 1, at] * fold(u3 * response)
            sum_z = sum_z + v.u2[y : y + 1, at] * fold(d3 * response)
        v.message[tile, 1:2, :] = jnp.sum(sum_y, axis=0, keepdims=True) * GRAD_SCALE
        v.message[tile, 2:3, :] = jnp.sum(sum_z, axis=0, keepdims=True) * GRAD_SCALE


SCRATCH = dict(
    pos=((3, CAP), F32), feat=((CAP, 128), BF16), cw=((CH, 128), BF16), ids=((1, CAP), jnp.int32),
    cot=((1, MOLS), F32), fin=((16, HID), BF16), fmid=((HID, HID), BF16), fout=((CH, HID), BF16),
    signs=((2 * HALF, YZ), BF16), signs_t=((YZ, 2 * HALF), BF16), lattice=((RING, 3, 1024), jnp.int32),
    u1=((8, CAP), F32), u2=((24, CAP), F32), u3=((24, CAP), F32), d2=((24, CAP), F32),
    alive=((1, CAP), F32), weight=((1, CAP), F32), member=((MOLS, CAP), BF16),
    pair=((2 * CH, CAP), BF16), b=((YZ, CAP), BF16), a=((XC, CAP), BF16), acc=((YZ, XC), F32),
    part=((2 * YZ, 128), BF16), mate=((YZ, 128), BF16), half=((YZ, 128), BF16),
    inbox=((CHIPS, BIG, 128), BF16), total=((2 * YZ, 128), BF16),
    radial=((TABLE, 16), BF16), act_one=((TABLE, HID), BF16), act_two=((TABLE, HID), BF16),
    slope_one=((TABLE, HID), F32), slope_two=((TABLE, HID), F32), fout_wide=((HID, 128), BF16),
    sigmoid=((TABLE, 128), F32), same=((TABLE, 2 * HALF), BF16), filters=((HALF, 128), F32),
    both=((HALF, 128), F32), difference=((HALF, 128), F32),
    sums=((2 * HALF, XC), F32), coef=((2 * HALF, XC), BF16), energy=((1, CAP), F32), cot_rows=((CH, CAP), BF16),
    gt=((XC, YZ), BF16), gs=((YZ, XC), BF16), response=((YZ, CAP), F32),
    up=((128, 128), BF16), up_ring=((RING, 64, 128), BF16), up_total=((128, 128), BF16),
    message=((RING, 4, TILE), F32), message_box=((RING, 4, TILE), F32),
    charge_ring=((RING, CH, 128), BF16), charge_mine=((CH, 128), BF16), charge_mate=((CH, 128), BF16),
    charge_plane=((CHIPS, CH, 128), BF16),
    mol_sum=((1, MOLS), F32), pos_sum=((3, TILE), F32), charge_sum=((CH, 128), F32),
    in_grad=((16, HID), F32), mid_grad=((HID, HID), F32), out_grad=((CH, HID), F32),
)
SEMAPHORES = dict(
    load=11, store=6, mate_s=4, mate_r=4, scatter_s=1, scatter_r=1, gather_s=1, gather_r=1,
    ring_s=4, ring_r=4, plane_s=1, plane_r=1,
)
OUTS = (
    ((1, MOLS), F32), ((3, TILE), F32), ((CH, 128), F32), ((16, HID), F32), ((HID, HID), F32), ((CH, HID), F32),
)


class Names:
    def __init__(self, names, refs):
        for name, ref in zip(names, refs, strict=True):
            setattr(self, name, ref)


def whole_kernel(
    count_ref, pos_ref, feat_ref, cw_ref, ids_ref, cot_ref, lattice_ref, fin_ref, fmid_ref, fout_ref,
    signs_ref, signs_t_ref, mol_out, pos_out, charge_out, in_out, mid_out, out_out, *scratch,
):
    v = Names(SCRATCH, scratch[: len(SCRATCH)])
    sem = Names(SEMAPHORES, scratch[len(SCRATCH) :])
    plane, ring = lax.axis_index("atoms"), lax.axis_index("kvec")
    chip, core = plane // 2, lax.rem(plane, 2)
    rank = ring

    loads = [
        pltpu.make_async_copy(src, dst, sem.load.at[i])
        for i, (src, dst) in enumerate((
            (pos_ref, v.pos), (feat_ref, v.feat), (cw_ref, v.cw), (ids_ref, v.ids), (cot_ref, v.cot),
            (lattice_ref, v.lattice.at[ring]), (fin_ref, v.fin), (fmid_ref, v.fmid), (fout_ref, v.fout),
            (signs_ref, v.signs), (signs_t_ref, v.signs_t),
        ))
    ]
    for load in loads:
        load.start()
    stores = [
        pltpu.make_async_copy(src, dst, sem.store.at[i])
        for i, (src, dst) in enumerate((
            (v.mol_sum, mol_out), (v.pos_sum, pos_out), (v.charge_sum, charge_out),
            (v.in_grad, in_out), (v.mid_grad, mid_out), (v.out_grad, out_out),
        ))
    ]

    def remote(src, dst, send, recv, device):
        return pltpu.make_async_remote_copy(
            src_ref=src, dst_ref=dst, send_sem=send, recv_sem=recv,
            device_id=device, device_id_type=MESH,
        )

    def await_bytes(ref, semaphore):
        pltpu.make_async_copy(ref, ref, semaphore).wait()

    def ring_peer(i):
        return (plane, lax.rem(ring + i, RING))

    def chip_device(which):
        return (2 * which + core, ring)

    mate = (plane + 1 - 2 * core, ring)

    barrier = pltpu.get_barrier_semaphore()

    def greet(device):
        pl.semaphore_signal(barrier, inc=1, device_id=device, device_id_type=MESH)

    loop(1, CHIPS, lambda i: greet(chip_device(lax.rem(chip + i, CHIPS))))
    loop(1, RING, lambda i: greet(ring_peer(i)))
    greet(mate)

    for load in loads[:5]:
        load.wait()
    first_pass(rank, count_ref[0], v, 0)
    for load in loads[5:]:
        load.wait()
    pl.semaphore_wait(barrier, CHIPS + RING - 1)

    def share(slots, phase):
        for i in FAR_FIRST:
            remote(slots.at[ring], slots.at[ring], sem.ring_s.at[phase], sem.ring_r.at[phase], ring_peer(i)).start()

    def shared(slots, phase):
        await_bytes(slots.at[pl.ds(0, RING - 1)], sem.ring_r.at[phase])

    share(v.lattice, 0)
    v.acc[...] = structure_sum(v, 0)
    first_pass(rank, count_ref[0], v, 1)
    structure = v.acc[...] + structure_sum(v, 1)
    v.part[:YZ, :] = structure[:, :128].astype(BF16)
    v.part[YZ:, :] = structure[:, 128:].astype(BF16)

    def half_rows(which):
        return pl.ds(pl.multiple_of(YZ * which, YZ), YZ)

    def to_mate(src, dst, phase):
        return remote(src, dst, sem.mate_s.at[phase], sem.mate_r.at[phase], mate)

    swap_parts = to_mate(v.part.at[half_rows(1 - core)], v.mate, 0)
    swap_parts.start()
    swap_parts.wait_recv()
    v.half[...] = (v.part[half_rows(core)].astype(F32) + v.mate[...].astype(F32)).astype(BF16)

    def pair_rows(which, odd, base=0):
        start = base + PAIR_ROWS * which + (BIG if odd else 0)
        return pl.ds(pl.multiple_of(start, 16), SMALL if odd else BIG)

    def scatter(pair, odd):
        size = SMALL if odd else BIG
        remote(
            v.half.at[pair_rows(pair, odd)], v.inbox.at[chip, pl.ds(0, size)],
            sem.scatter_s.at[0], sem.scatter_r.at[0], chip_device(2 * pair + odd),
        ).start()

    my_pair, my_odd = chip // 2, lax.rem(chip, 2)

    def scatter_pair(i):
        pair = lax.rem(my_pair + 1 + lax.rem(i + 3, 7), 8)
        scatter(pair, 0)
        scatter(pair, 1)

    loop(0, 7, scatter_pair)
    pl.when(my_odd == 0)(lambda: scatter(my_pair, 1))
    pl.when(my_odd == 1)(lambda: scatter(my_pair, 0))
    filter_forward(rank, v)
    table_forward(rank, v)

    def reduce(odd):
        size = SMALL if odd else BIG
        v.inbox[chip, :size] = v.half[pair_rows(my_pair, odd)]
        await_bytes(v.inbox.at[pl.ds(0, CHIPS - 1), pl.ds(0, size)], sem.scatter_r.at[0])
        value = v.inbox[0, :size].astype(F32)
        for slot in range(1, CHIPS):
            value = value + v.inbox[slot, :size].astype(F32)
        rows = pair_rows(my_pair, odd, YZ * core)
        v.total[rows] = value.astype(BF16)

        def send(i):
            other = lax.rem(chip + 1 + lax.rem(i + 5, 15), CHIPS)
            remote(
                v.total.at[rows], v.total.at[rows], sem.gather_s.at[0], sem.gather_r.at[0],
                chip_device(other),
            ).start()

        loop(0, CHIPS - 1, send)

    pl.when(my_odd == 0)(lambda: reduce(0))
    pl.when(my_odd == 1)(lambda: reduce(1))

    shared(v.lattice, 0)
    multiplicities(rank, v)

    def reduced(odd):
        size = SMALL if odd else BIG
        await_bytes(v.total.at[pl.ds(0, YZ - size)], sem.gather_r.at[0])
        await_bytes(v.total.at[pl.ds(0, YZ - size)], sem.scatter_s.at[0])

    pl.when(my_odd == 0)(lambda: reduced(0))
    pl.when(my_odd == 1)(lambda: reduced(1))
    swap_totals = to_mate(v.total.at[half_rows(core)], v.total.at[half_rows(core)], 1)
    swap_totals.start()
    swap_totals.wait_recv()

    coefficients(v)
    v.up[...] = upstream_table(v)
    v.up_ring[ring] = v.up[pl.ds(pl.multiple_of(64 * core, 64), 64), :]
    share(v.up_ring, 1)
    v.charge_ring[ring] = potential_pass(rank, v).astype(BF16)
    share(v.charge_ring, 2)
    molecules = molecule_sums(v)
    for chunk in range(RING):
        v.message[chunk, 3:4, 0:MOLS] = molecules
        v.message[chunk, 3:4, MOLS:TILE] = jnp.zeros((1, TILE - MOLS), F32)

    swapped_coefficients(v)
    force_pass(v)
    for i in FAR_FIRST:
        peer = lax.rem(ring + i, RING)
        remote(v.message.at[peer], v.message_box.at[ring], sem.ring_s.at[3], sem.ring_r.at[3], ring_peer(i)).start()
    v.message_box[ring] = v.message[ring]

    def added(slots):
        value = slots[0].astype(F32)
        for slot in range(1, slots.shape[0]):
            value = value + slots[slot].astype(F32)
        return value

    shared(v.up_ring, 1)
    up_rows = pl.ds(pl.multiple_of(64 * core, 64), 64)
    v.up_total[up_rows, :] = added(v.up_ring).astype(BF16)
    swap_up = to_mate(v.up_total.at[up_rows], v.up_total.at[up_rows], 2)
    swap_up.start()

    shared(v.charge_ring, 2)
    v.charge_mine[...] = added(v.charge_ring).astype(BF16)
    swap_charge = to_mate(v.charge_mine, v.charge_mate, 3)
    swap_charge.start()
    swap_charge.wait_recv()
    v.charge_plane[chip] = (v.charge_mine[...].astype(F32) + v.charge_mate[...].astype(F32)).astype(BF16)

    def charge_to_plane(i):
        other = lax.rem(chip + 1 + lax.rem(i + 5, 15), CHIPS)
        remote(
            v.charge_plane.at[chip], v.charge_plane.at[chip], sem.plane_s.at[0], sem.plane_r.at[0],
            chip_device(other),
        ).start()

    loop(0, CHIPS - 1, charge_to_plane)

    swap_up.wait_recv()
    filter_backward(v)
    for store in stores[3:]:
        store.start()
    shared(v.message_box, 3)
    value = added(v.message_box)
    v.pos_sum[...] = value[0:3]
    v.mol_sum[...] = value[3:4, :MOLS]
    for store in stores[:2]:
        store.start()

    for swap in (swap_parts, swap_totals, swap_up, swap_charge):
        swap.wait_send()
    for phase, slots in enumerate((v.lattice, v.up_ring, v.charge_ring, v.message)):
        await_bytes(slots.at[pl.ds(0, RING - 1)], sem.ring_s.at[phase])

    def gathered(odd):
        size = SMALL if odd else BIG
        await_bytes(v.inbox.at[pl.ds(0, CHIPS - 1), pl.ds(0, size)], sem.gather_s.at[0])

    pl.when(my_odd == 0)(lambda: gathered(0))
    pl.when(my_odd == 1)(lambda: gathered(1))
    await_bytes(v.charge_plane.at[pl.ds(0, CHIPS - 1)], sem.plane_s.at[0])

    await_bytes(v.charge_plane.at[pl.ds(0, CHIPS - 1)], sem.plane_r.at[0])
    v.charge_sum[...] = added(v.charge_plane)
    stores[2].start()
    for store in stores:
        store.wait()


def output_kernel(*refs):
    count = len(OUTS)
    sem = refs[-1]
    copies = [pltpu.make_async_copy(refs[i], refs[count + i], sem.at[i]) for i in range(count)]
    for copy in copies:
        copy.start()
    for copy in copies:
        copy.wait()


def specs(space, count):
    return [pl.BlockSpec(memory_space=space)] * count


def body(
    positions, features, charge_weight, counts, mol_ids, energy_cot,
    lattice, filter_in, filter_mid, filter_out,
):
    shape = jax.ShapeDtypeStruct
    dma = pltpu.SemaphoreType.DMA
    signs = jnp.asarray(sign_matrix(), BF16)
    signs_t = jnp.asarray(sign_matrix().T, BF16)
    outs = tuple(shape(*out) for out in OUTS)
    sums = pl.pallas_call(
        whole_kernel,
        out_shape=outs,
        in_specs=specs(pltpu.SMEM, 1) + specs(pl.ANY, 11),
        out_specs=tuple(specs(pl.ANY, len(OUTS))),
        scratch_shapes=[pltpu.VMEM(dims, kind) for dims, kind in SCRATCH.values()]
        + [dma((count,)) for count in SEMAPHORES.values()],
        compiler_params=pltpu.CompilerParams(
            collective_id=0, has_side_effects=True, vmem_limit_bytes=56 * MIB
        ),
        name="ewald",
    )(
        counts, positions, features, charge_weight.T, mol_ids, energy_cot.reshape(1, MOLS), lattice,
        filter_in, filter_mid, filter_out.T, signs, signs_t,
    )
    mol, pos, charge, first, middle, last = pl.pallas_call(
        output_kernel,
        out_shape=outs,
        in_specs=specs(pl.ANY, len(OUTS)),
        out_specs=tuple(specs(pl.ANY, len(OUTS))),
        scratch_shapes=[dma((len(OUTS),))],
        compiler_params=pltpu.CompilerParams(vmem_limit_bytes=56 * MIB),
        name="outputs",
    )(*sums)
    return (mol.reshape(MOLS), pos, charge.T, first, middle, last.T)


def solution(mesh):
    return jax.shard_map(
        body,
        mesh=mesh,
        in_specs=(
            P(None, "atoms"), P("atoms", None), P(), P("atoms"), P("atoms", None), P("atoms"),
            P(None, "kvec"), P(), P(), P(),
        ),
        out_specs=(P("atoms"), P(None, ("atoms", "kvec")), P(), P(), P(), P()),
        check_vma=False,
    )
```

```python
import functools
import math

import jax
import jax.numpy as jnp
import numpy as np
from jax import lax
from jax.experimental import pallas as pl
from jax.experimental.pallas import tpu as pltpu
from jax.sharding import PartitionSpec as P

MAXN = 12
BOX_EDGE = 40.0
MESH = pl.DeviceIdType.MESH
F32 = jnp.float32
BF16 = jnp.bfloat16

PLANE = 32
RING = 8
CAP = 4096
CH = 32
HID = 256
MOLS = 256
YZ = 640
XC = 256
HALF = 320
TILE = 512
TILES = CAP // TILE
CHIPS = 16
PAIR_ROWS = 80
BIG = 48
SMALL = 32
TABLE = 512
FAR_FIRST = (4, 3, 5, 2, 6, 1, 7)
MIB = 1 << 20


def row_of(y_index, z_index):
    if y_index is None and z_index is None:
        return 624
    if y_index is None:
        return 576 + z_index
    if z_index is None:
        return 600 + y_index
    return 24 * y_index + z_index


def half_plane():
    vectors = [(0, n3) for n3 in range(13)]
    return vectors + [(n2, n3) for n2 in range(1, 13) for n3 in range(-12, 13)]


def sign_matrix():
    def cosine(n):
        return None if n == 0 else n - 1

    def sine(n):
        return 12 + n - 1

    matrix = np.zeros((2 * HALF, YZ), np.float32)
    for index, (n2, n3) in enumerate(half_plane()):
        size, sign = abs(n3), (1.0 if n3 >= 0 else -1.0)
        matrix[index, row_of(cosine(n2), cosine(size))] = 1.0
        if n2 and size:
            matrix[index, row_of(sine(n2), sine(size))] = -sign
        if n2:
            matrix[HALF + index, row_of(sine(n2), cosine(size))] = 1.0
        if size:
            matrix[HALF + index, row_of(cosine(n2), sine(size))] = sign
    return matrix


def nt(first, second):
    return lax.dot_general(first, second, (((1,), (1,)), ((), ())), preferred_element_type=F32)


def tn(first, second):
    return lax.dot_general(first, second, (((0,), (0,)), ((), ())), preferred_element_type=F32)


def nn(first, second):
    return jnp.dot(first, second, preferred_element_type=F32)


def cos_turns(turns):
    frac = turns - jnp.floor(turns + 0.5)
    x = (2.0 * math.pi) * (0.25 - jnp.abs(frac))
    s = x * x
    poly = jnp.full_like(s, -1.0 / 39916800.0)
    for coefficient in (1.0 / 362880.0, -1.0 / 5040.0, 1.0 / 120.0, -1.0 / 6.0, 1.0):
        poly = poly * s + coefficient
    return x * poly


def rows_of_parts(value):
    high = value.astype(BF16).astype(F32)
    rest = value - high
    middle = rest.astype(BF16).astype(F32)
    low = rest - middle
    row = lax.broadcasted_iota(jnp.int32, (16, value.shape[1]), 0)
    parts = jnp.where(row == 0, high, jnp.where(row == 1, middle, jnp.where(row == 2, low, 0.0)))
    return parts.astype(BF16)


def yz_turns(coord):
    row = lax.broadcasted_iota(jnp.int32, (24, 1), 0)
    harmonic = jnp.where(row < 12, row + 1, row - 11).astype(F32)
    shift = jnp.where(row < 12, 0.0, 0.25)
    return harmonic * coord - shift, harmonic


def x_turns(coord, rank):
    row = lax.broadcasted_iota(jnp.int32, (8, 1), 0)
    harmonic = (2 * rank + lax.rem(row, 2)).astype(F32)
    shift = jnp.where(row < 2, 0.0, 0.25)
    return harmonic * coord - shift, harmonic


def lane_roll(value, shift):
    return pltpu.roll(value, shift % value.shape[1], 1)


def slope(preact, sigmoid_val):
    return sigmoid_val * (1.0 + preact * (1.0 - sigmoid_val))


def point_squares(rank, axis):
    dims = (2 * HALF, 1) if axis == 0 else (1, 2 * HALF)
    index = lax.broadcasted_iota(jnp.int32, dims, axis)
    n1 = (2 * rank + jnp.where(index >= HALF, 1, 0)).astype(F32)
    index = jnp.where(index >= HALF, index - HALF, index)
    later = (index - 13).astype(F32)
    n2 = jnp.where(index < 13, 0.0, 1.0 + jnp.floor((later + 0.5) * (1.0 / 25.0)))
    n3 = jnp.where(index < 13, index.astype(F32), later - 25.0 * (n2 - 1.0) - 12.0)
    return n1 * n1 + n2 * n2 + n3 * n3


def loop(low, high, action):
    def run(i, carry):
        action(i)
        return carry

    lax.fori_loop(low, high, run, 0)


def first_pass(rank, count, v, half):
    cot_parts = rows_of_parts(v.cot[...])
    for tile in range(half * TILES // 2, (half + 1) * TILES // 2):
        at = pl.ds(tile * TILE, TILE)
        slot = tile * TILE + lax.broadcasted_iota(jnp.int32, (1, TILE), 1)
        alive = jnp.where(slot < count, 1.0, 0.0)
        v.alive[:, at] = alive
        molecule = lax.broadcasted_iota(jnp.int32, (MOLS, TILE), 0)
        member = jnp.where(molecule == v.ids[:, at], 1.0, 0.0).astype(BF16)
        v.member[:, at] = member
        weight = jnp.sum(nn(cot_parts, member), axis=0, keepdims=True)
        v.weight[:, at] = weight
        charge = (nt(v.cw[...], v.feat[at, :]) * alive).astype(BF16).astype(F32)
        pair = jnp.concatenate([charge, weight * charge], axis=0).astype(BF16)
        v.pair[:, at] = pair
        pair = pair.astype(F32)
        turns2, _ = yz_turns(v.pos[1:2, at])
        turns3, _ = yz_turns(v.pos[2:3, at])
        turns1, _ = x_turns(v.pos[0:1, at], rank)
        v.u2[:, at] = cos_turns(turns2)
        v.u3[:, at] = cos_turns(turns3)
        v.u1[:, at] = cos_turns(turns1)
        u3 = v.u3[:, at]
        for two in range(12):
            first = v.u2[2 * two : 2 * two + 1, at] * u3
            second = v.u2[2 * two + 1 : 2 * two + 2, at] * u3
            rows = jnp.concatenate([first, second], axis=0).astype(BF16)
            v.b[48 * two : 48 * two + 48, at] = rows
        v.b[576:624, at] = jnp.concatenate([u3, v.u2[:, at]], axis=0).astype(BF16)
        row = lax.broadcasted_iota(jnp.int32, (16, TILE), 0)
        v.b[624:640, at] = jnp.where(row == 0, 1.0, 0.0).astype(BF16)
        for j in range(4):
            v.a[64 * j : 64 * j + 64, at] = (v.u1[j : j + 1, at] * pair).astype(BF16)


def structure_sum(v, rows, half):
    at = pl.ds(half * CAP // 2, CAP // 2)
    return nt(v.b[rows, at], v.a[:, at])


def network(squared, v):
    inverse = jnp.where(squared > 0.0, 1.0, 0.0) / (
        jnp.maximum(squared, 1.0) * math.sqrt(CAP * PLANE)
    )
    spacing = MAXN * math.sqrt(3.0) / 16
    center = (lax.broadcasted_iota(jnp.int32, (1, 16), 1).astype(F32) + 0.5) * spacing
    away = (jnp.sqrt(squared) - center) / spacing
    radial = jnp.exp(-0.5 * away * away).astype(BF16)
    pre_one = nn(radial, v.fin[...])
    sig_one = jax.nn.sigmoid(pre_one)
    act_one = (pre_one * sig_one).astype(BF16)
    pre_two = nn(act_one, v.fmid[...])
    sig_two = jax.nn.sigmoid(pre_two)
    act_two = (pre_two * sig_two).astype(BF16)
    logits = nn(act_two, v.fout_wide[...])
    return inverse, radial, pre_one, sig_one, act_one, pre_two, sig_two, act_two, logits


def filter_forward(rank, v):
    lane = lax.broadcasted_iota(jnp.int32, (CH, 128), 1)
    channel = lax.broadcasted_iota(jnp.int32, (CH, 128), 0)
    spread = jnp.where(lax.rem(lane, CH) == channel, 1.0, 0.0).astype(BF16)
    v.fout_wide[...] = tn(v.fout[...], spread).astype(BF16)
    values = network(point_squares(rank, 0), v)
    inverse, logits = values[0], values[-1]
    soft = jnp.maximum(logits, 0.0) + jnp.log1p(jnp.exp(-jnp.abs(logits)))
    soft = soft * inverse
    half_lane = lax.broadcasted_iota(jnp.int32, (HALF, 128), 1)
    v.filters[...] = jnp.where(half_lane < 64, soft[:HALF], soft[HALF:])


def table_forward(rank, v):
    table = lax.broadcasted_iota(jnp.int32, (TABLE, 1), 0).astype(F32)
    inverse, radial, pre_one, sig_one, act_one, pre_two, sig_two, act_two, logits = network(table, v)
    v.radial[...] = radial
    v.act_one[...] = act_one
    v.act_two[...] = act_two
    v.slope_one[...] = slope(pre_one, sig_one)
    v.slope_two[...] = slope(pre_two, sig_two)
    v.sigmoid[...] = jax.nn.sigmoid(logits) * inverse
    v.same[...] = jnp.where(table == point_squares(rank, 1), 1.0, 0.0).astype(BF16)


def multiplicities(rank, v):
    def chunk(index, total):
        k = v.lattice[index]
        k1, k2, k3 = k[0:1, :], k[1:2, :], k[2:3, :]
        back = k1 < 0
        k1 = jnp.where(back, -k1, k1)
        k2 = jnp.where(back, -k2, k2)
        k3 = jnp.where(back, -k3, k3)
        flip = (k2 < 0) | ((k2 == 0) & (k3 < 0))
        k2 = jnp.where(flip, -k2, k2)
        k3 = jnp.where(flip, -k3, k3)
        code = jnp.where(k2 == 0, k3, k2 * 25 + k3)
        width = k.shape[1]
        hit = lax.broadcasted_iota(jnp.int32, (HALF, width), 0) == code
        hit = jnp.where(hit, 1.0, 0.0).astype(BF16)
        row = lax.broadcasted_iota(jnp.int32, (16, width), 0)
        own = (k1 - 2 * rank) == lax.rem(row, 2)
        sign = jnp.where((row >= 2) & flip, -1.0, 1.0)
        select = jnp.where(own & (row < 4), sign, 0.0).astype(BF16)
        return total + nt(hit, select)

    counted = lax.fori_loop(0, RING, chunk, jnp.zeros((HALF, 16), F32))
    lane = lax.broadcasted_iota(jnp.int32, (HALF, 128), 1)
    v.both[...] = jnp.where(lane < 64, counted[:, 0:1], counted[:, 1:2])
    v.difference[...] = jnp.where(lane < 64, counted[:, 2:3], counted[:, 3:4])


def coefficients(v):
    signs = v.signs[...]
    total = jnp.concatenate(
        [
            jnp.concatenate([v.total[start : start + HALF], v.total[start + HALF : start + YZ]], axis=1)
            for start in (0, YZ)
        ],
        axis=0,
    )
    v.sums[...] = nn(signs, total)
    ncc, ncs = v.sums[:HALF, :128], v.sums[HALF:, :128]
    nsc, nss = v.sums[:HALF, 128:], v.sums[HALF:, 128:]
    filters = v.filters[...]
    fp, fd = filters * v.both[...], filters * v.difference[...]
    gcc = (fp * ncc - fd * nss).astype(BF16)
    gss = (fp * nss - fd * ncc).astype(BF16)
    gsc = (fp * nsc + fd * ncs).astype(BF16)
    gcs = (fp * ncs + fd * nsc).astype(BF16)
    v.coef[:HALF, :128] = gcc
    v.coef[HALF:, :128] = gcs
    v.coef[:HALF, 128:] = gsc
    v.coef[HALF:, 128:] = gss
    v.gt[...] = tn(v.coef[...], signs).astype(BF16)


def swapped_coefficients(v):
    g = nn(v.signs_t[...], v.coef[...])
    lane = lax.broadcasted_iota(jnp.int32, (YZ, XC), 1)
    swapped = jnp.where(lax.rem(lane, 64) < 32, lane_roll(g, -32), lane_roll(g, 32))
    v.gs[...] = swapped.astype(BF16)


def upstream_table(v):
    ncc, ncs = v.sums[:HALF, :128], v.sums[HALF:, :128]
    nsc, nss = v.sums[:HALF, 128:], v.sums[HALF:, 128:]
    tcc, tcs = lane_roll(ncc, -32), lane_roll(ncs, -32)
    tsc, tss = lane_roll(nsc, -32), lane_roll(nss, -32)
    upstream = 0.5 * (
        v.both[...] * (ncc * tcc + nss * tss + nsc * tsc + ncs * tcs)
        + v.difference[...] * (nsc * tcs + ncs * tsc - ncc * tss - nss * tcc)
    )
    upstream = jnp.concatenate([upstream, lane_roll(upstream, -64)], axis=0)
    lane = lax.broadcasted_iota(jnp.int32, (2 * HALF, 128), 1)
    upstream = jnp.where(lane < CH, upstream, 0.0)
    total = nn(v.same[0:128, :], upstream.astype(BF16))
    for group in range(1, 4):
        rows = v.same[128 * group : 128 * group + 128, :]
        total = total + nn(rows, lane_roll(upstream, 32 * group).astype(BF16))
    return total.astype(BF16)


def filter_backward(v):
    upstream = v.up_total[...].astype(F32)
    upstream = jnp.concatenate(
        [upstream] + [lane_roll(upstream, -32 * group) for group in range(1, 4)], axis=0
    )
    lane = lax.broadcasted_iota(jnp.int32, (TABLE, 128), 1)
    grad_logits = jnp.where(lane < CH, upstream * v.sigmoid[...], 0.0).astype(BF16)
    out_grad = tn(grad_logits, v.act_two[...])
    grad_two = (nt(grad_logits, v.fout_wide[...]) * v.slope_two[...]).astype(BF16)
    v.mid_grad[...] = tn(v.act_one[...], grad_two)
    grad_one = (nt(grad_two, v.fmid[...]) * v.slope_one[...]).astype(BF16)
    v.in_grad[...] = tn(v.radial[...], grad_one)
    v.out_grad[...] = out_grad[:CH]


GRAD_SCALE = 0.5 * 2.0 * math.pi / BOX_EDGE


def potential_pass(rank, v):
    for tile in range(TILES):
        at = pl.ds(tile * TILE, TILE)
        turns1, h1 = x_turns(v.pos[0:1, at], rank)
        d1 = h1 * cos_turns(turns1 + 0.25)
        u1 = v.u1[:, at]
        pair = v.pair[:, at].astype(F32)
        charge, weighted = pair[:CH], pair[CH:]
        w = nn(v.gt[...], v.b[:, at])
        pot = sum(u1[j : j + 1, :] * w[64 * j : 64 * j + 64, :] for j in range(4))
        potx = sum(d1[j : j + 1, :] * w[64 * j : 64 * j + 64, :] for j in range(4))
        volt, other = pot[:CH], pot[CH:]
        grad_x = jnp.sum(weighted * potx[:CH] + charge * potx[CH:], axis=0, keepdims=True)
        v.message[tile, 0:1, :] = grad_x * GRAD_SCALE
        v.energy[:, at] = 0.5 * jnp.sum(charge * volt, axis=0, keepdims=True)
        v.cot_rows[:, at] = (0.5 * (v.weight[:, at] * volt + other) * v.alive[:, at]).astype(BF16)
    return nn(v.cot_rows[...], v.feat[...])


def molecule_sums(v):
    return jnp.sum(nt(rows_of_parts(v.energy[...]), v.member[...]), axis=0, keepdims=True)


def force_pass(v):
    def fold(value):
        return value[0:8] + value[8:16] + value[16:24]

    for tile in range(TILES):
        at = pl.ds(tile * TILE, TILE)
        turns2, h2 = yz_turns(v.pos[1:2, at])
        turns3, h3 = yz_turns(v.pos[2:3, at])
        v.d2[:, at] = h2 * cos_turns(turns2 + 0.25)
        v.response[:, at] = nn(v.gs[...], v.a[:, at])
        u3, d3 = v.u3[:, at], h3 * cos_turns(turns3 + 0.25)
        sum_y = fold(v.d2[:, at] * v.response[600:624, at])
        sum_z = fold(d3 * v.response[576:600, at])
        for y in range(24):
            response = v.response[24 * y : 24 * y + 24, at]
            sum_y = sum_y + v.d2[y : y + 1, at] * fold(u3 * response)
            sum_z = sum_z + v.u2[y : y + 1, at] * fold(d3 * response)
        v.message[tile, 1:2, :] = jnp.sum(sum_y, axis=0, keepdims=True) * GRAD_SCALE
        v.message[tile, 2:3, :] = jnp.sum(sum_z, axis=0, keepdims=True) * GRAD_SCALE


SCRATCH = dict(
    pos=((3, CAP), F32), feat=((CAP, 128), BF16), cw=((CH, 128), BF16), ids=((1, CAP), jnp.int32),
    cot=((1, MOLS), F32), fin=((16, HID), BF16), fmid=((HID, HID), BF16), fout=((CH, HID), BF16),
    signs=((2 * HALF, YZ), BF16), signs_t=((YZ, 2 * HALF), BF16), lattice=((RING, 3, 1024), jnp.int32),
    u1=((8, CAP), F32), u2=((24, CAP), F32), u3=((24, CAP), F32), d2=((24, CAP), F32),
    alive=((1, CAP), F32), weight=((1, CAP), F32), member=((MOLS, CAP), BF16),
    pair=((2 * CH, CAP), BF16), b=((YZ, CAP), BF16), a=((XC, CAP), BF16), acc=((YZ, XC), F32),
    part=((YZ, 128), BF16), mate=((YZ, 128), BF16), half=((YZ, 128), BF16),
    inbox=((CHIPS, BIG, 128), BF16), total=((2 * YZ, 128), BF16),
    radial=((TABLE, 16), BF16), act_one=((TABLE, HID), BF16), act_two=((TABLE, HID), BF16),
    slope_one=((TABLE, HID), F32), slope_two=((TABLE, HID), F32), fout_wide=((HID, 128), BF16),
    sigmoid=((TABLE, 128), F32), same=((TABLE, 2 * HALF), BF16), filters=((HALF, 128), F32),
    both=((HALF, 128), F32), difference=((HALF, 128), F32),
    sums=((2 * HALF, XC), F32), coef=((2 * HALF, XC), BF16), energy=((1, CAP), F32), cot_rows=((CH, CAP), BF16),
    gt=((XC, YZ), BF16), gs=((YZ, XC), BF16), response=((YZ, CAP), F32),
    up=((128, 128), BF16), up_ring=((RING, 64, 128), BF16), up_total=((128, 128), BF16),
    message=((RING, 4, TILE), F32), message_box=((RING, 4, TILE), F32),
    charge_ring=((RING, CH, 128), BF16), charge_mine=((CH, 128), BF16), charge_mate=((CH, 128), BF16),
    charge_plane=((CHIPS, CH, 128), BF16),
    mol_sum=((1, MOLS), F32), pos_sum=((3, TILE), F32), charge_sum=((CH, 128), F32),
    in_grad=((16, HID), F32), mid_grad=((HID, HID), F32), out_grad=((CH, HID), F32),
)
SEMAPHORES = dict(
    load=11, store=6, mate_s=4, mate_r=4, scatter_s=1, scatter_r=1, gather_s=1, gather_r=1,
    ring_s=4, ring_r=4, plane_s=1, plane_r=1,
)
OUTS = (
    ((1, MOLS), F32), ((3, TILE), F32), ((CH, 128), F32), ((16, HID), F32), ((HID, HID), F32), ((CH, HID), F32),
)


class Names:
    def __init__(self, names, refs):
        for name, ref in zip(names, refs, strict=True):
            setattr(self, name, ref)


def whole_kernel(
    count_ref, pos_ref, feat_ref, cw_ref, ids_ref, cot_ref, lattice_ref, fin_ref, fmid_ref, fout_ref,
    signs_ref, signs_t_ref, mol_out, pos_out, charge_out, in_out, mid_out, out_out, *scratch,
):
    v = Names(SCRATCH, scratch[: len(SCRATCH)])
    sem = Names(SEMAPHORES, scratch[len(SCRATCH) :])
    plane, ring = lax.axis_index("atoms"), lax.axis_index("kvec")
    chip, core = plane // 2, lax.rem(plane, 2)
    rank = ring

    loads = [
        pltpu.make_async_copy(src, dst, sem.load.at[i])
        for i, (src, dst) in enumerate((
            (pos_ref, v.pos), (feat_ref, v.feat), (cw_ref, v.cw), (ids_ref, v.ids), (cot_ref, v.cot),
            (lattice_ref, v.lattice.at[ring]), (fin_ref, v.fin), (fmid_ref, v.fmid), (fout_ref, v.fout),
            (signs_ref, v.signs), (signs_t_ref, v.signs_t),
        ))
    ]
    for load in loads:
        load.start()
    stores = [
        pltpu.make_async_copy(src, dst, sem.store.at[i])
        for i, (src, dst) in enumerate((
            (v.mol_sum, mol_out), (v.pos_sum, pos_out), (v.charge_sum, charge_out),
            (v.in_grad, in_out), (v.mid_grad, mid_out), (v.out_grad, out_out),
        ))
    ]

    def remote(src, dst, send, recv, device):
        return pltpu.make_async_remote_copy(
            src_ref=src, dst_ref=dst, send_sem=send, recv_sem=recv,
            device_id=device, device_id_type=MESH,
        )

    def await_bytes(ref, semaphore):
        pltpu.make_async_copy(ref, ref, semaphore).wait()

    def ring_peer(i):
        return (plane, lax.rem(ring + i, RING))

    def chip_device(which):
        return (2 * which + core, ring)

    mate = (plane + 1 - 2 * core, ring)

    barrier = pltpu.get_barrier_semaphore()

    def greet(device):
        pl.semaphore_signal(barrier, inc=1, device_id=device, device_id_type=MESH)

    loop(1, CHIPS, lambda i: greet(chip_device(lax.rem(chip + i, CHIPS))))
    loop(1, RING, lambda i: greet(ring_peer(i)))
    greet(mate)

    for load in loads[:5]:
        load.wait()
    for half in range(2):
        first_pass(rank, count_ref[0], v, half)
        if half == 0:
            v.acc[...] = structure_sum(v, pl.ds(0, YZ), 0)

    def share(slots, phase):
        for i in FAR_FIRST:
            remote(slots.at[ring], slots.at[ring], sem.ring_s.at[phase], sem.ring_r.at[phase], ring_peer(i)).start()

    def shared(slots, phase):
        await_bytes(slots.at[pl.ds(0, RING - 1)], sem.ring_r.at[phase])

    def half_rows(which):
        return pl.ds(pl.multiple_of(YZ * which, YZ), YZ)

    def to_mate(src, dst, phase):
        return remote(src, dst, sem.mate_s.at[phase], sem.mate_r.at[phase], mate)

    def row_sums(which):
        rows = pl.ds(pl.multiple_of(HALF * which, HALF), HALF)
        return v.acc[rows, :] + structure_sum(v, rows, 1)

    theirs = row_sums(1 - core)
    v.part[:HALF, :] = theirs[:, :128].astype(BF16)
    v.part[HALF:, :] = theirs[:, 128:].astype(BF16)
    pl.semaphore_wait(barrier, CHIPS + RING - 1)
    swap_parts = to_mate(v.part, v.mate, 0)
    swap_parts.start()
    for load in loads[5:]:
        load.wait()
    share(v.lattice, 0)
    mine = row_sums(core)
    swap_parts.wait_recv()
    v.half[:HALF, :] = (mine[:, :128] + v.mate[:HALF, :].astype(F32)).astype(BF16)
    v.half[HALF:, :] = (mine[:, 128:] + v.mate[HALF:, :].astype(F32)).astype(BF16)

    def pair_rows(which, odd, base=0):
        start = base + PAIR_ROWS * which + (BIG if odd else 0)
        return pl.ds(pl.multiple_of(start, 16), SMALL if odd else BIG)

    def scatter(pair, odd):
        size = SMALL if odd else BIG
        remote(
            v.half.at[pair_rows(pair, odd)], v.inbox.at[chip, pl.ds(0, size)],
            sem.scatter_s.at[0], sem.scatter_r.at[0], chip_device(2 * pair + odd),
        ).start()

    my_pair, my_odd = chip // 2, lax.rem(chip, 2)

    def scatter_pair(i):
        pair = lax.rem(my_pair + 1 + lax.rem(i + 3, 7), 8)
        scatter(pair, 0)
        scatter(pair, 1)

    loop(0, 7, scatter_pair)
    pl.when(my_odd == 0)(lambda: scatter(my_pair, 1))
    pl.when(my_odd == 1)(lambda: scatter(my_pair, 0))
    filter_forward(rank, v)
    table_forward(rank, v)

    def reduce(odd):
        size = SMALL if odd else BIG
        v.inbox[chip, :size] = v.half[pair_rows(my_pair, odd)]
        await_bytes(v.inbox.at[pl.ds(0, CHIPS - 1), pl.ds(0, size)], sem.scatter_r.at[0])
        value = v.inbox[0, :size].astype(F32)
        for slot in range(1, CHIPS):
            value = value + v.inbox[slot, :size].astype(F32)
        rows = pair_rows(my_pair, odd, YZ * core)
        v.total[rows] = value.astype(BF16)

        def send(i):
            other = lax.rem(chip + 1 + lax.rem(i + 5, 15), CHIPS)
            remote(
                v.total.at[rows], v.total.at[rows], sem.gather_s.at[0], sem.gather_r.at[0],
                chip_device(other),
            ).start()

        loop(0, CHIPS - 1, send)

    pl.when(my_odd == 0)(lambda: reduce(0))
    pl.when(my_odd == 1)(lambda: reduce(1))

    shared(v.lattice, 0)
    multiplicities(rank, v)

    def reduced(odd):
        size = SMALL if odd else BIG
        await_bytes(v.total.at[pl.ds(0, YZ - size)], sem.gather_r.at[0])
        await_bytes(v.total.at[pl.ds(0, YZ - size)], sem.scatter_s.at[0])

    pl.when(my_odd == 0)(lambda: reduced(0))
    pl.when(my_odd == 1)(lambda: reduced(1))
    swap_totals = to_mate(v.total.at[half_rows(core)], v.total.at[half_rows(core)], 1)
    swap_totals.start()
    swap_totals.wait_recv()

    coefficients(v)
    v.charge_ring[ring] = potential_pass(rank, v).astype(BF16)
    share(v.charge_ring, 2)
    v.up[...] = upstream_table(v)
    v.up_ring[ring] = v.up[pl.ds(pl.multiple_of(64 * core, 64), 64), :]
    share(v.up_ring, 1)
    molecules = molecule_sums(v)
    for chunk in range(RING):
        v.message[chunk, 3:4, 0:MOLS] = molecules
        v.message[chunk, 3:4, MOLS:TILE] = jnp.zeros((1, TILE - MOLS), F32)

    swapped_coefficients(v)
    force_pass(v)
    for i in FAR_FIRST:
        peer = lax.rem(ring + i, RING)
        remote(v.message.at[peer], v.message_box.at[ring], sem.ring_s.at[3], sem.ring_r.at[3], ring_peer(i)).start()
    v.message_box[ring] = v.message[ring]

    def added(slots):
        value = slots[0].astype(F32)
        for slot in range(1, slots.shape[0]):
            value = value + slots[slot].astype(F32)
        return value

    shared(v.up_ring, 1)
    up_rows = pl.ds(pl.multiple_of(64 * core, 64), 64)
    v.up_total[up_rows, :] = added(v.up_ring).astype(BF16)
    swap_up = to_mate(v.up_total.at[up_rows], v.up_total.at[up_rows], 2)
    swap_up.start()

    shared(v.charge_ring, 2)
    v.charge_mine[...] = added(v.charge_ring).astype(BF16)
    swap_charge = to_mate(v.charge_mine, v.charge_mate, 3)
    swap_charge.start()
    swap_charge.wait_recv()
    v.charge_plane[chip] = (v.charge_mine[...].astype(F32) + v.charge_mate[...].astype(F32)).astype(BF16)

    def charge_to_plane(i):
        other = lax.rem(chip + 1 + lax.rem(i + 5, 15), CHIPS)
        remote(
            v.charge_plane.at[chip], v.charge_plane.at[chip], sem.plane_s.at[0], sem.plane_r.at[0],
            chip_device(other),
        ).start()

    loop(0, CHIPS - 1, charge_to_plane)

    swap_up.wait_recv()
    filter_backward(v)
    for store in stores[3:]:
        store.start()
    shared(v.message_box, 3)
    value = added(v.message_box)
    v.pos_sum[...] = value[0:3]
    v.mol_sum[...] = value[3:4, :MOLS]
    for store in stores[:2]:
        store.start()

    for swap in (swap_parts, swap_totals, swap_up, swap_charge):
        swap.wait_send()
    for phase, slots in enumerate((v.lattice, v.up_ring, v.charge_ring, v.message)):
        await_bytes(slots.at[pl.ds(0, RING - 1)], sem.ring_s.at[phase])

    def gathered(odd):
        size = SMALL if odd else BIG
        await_bytes(v.inbox.at[pl.ds(0, CHIPS - 1), pl.ds(0, size)], sem.gather_s.at[0])

    pl.when(my_odd == 0)(lambda: gathered(0))
    pl.when(my_odd == 1)(lambda: gathered(1))
    await_bytes(v.charge_plane.at[pl.ds(0, CHIPS - 1)], sem.plane_s.at[0])

    await_bytes(v.charge_plane.at[pl.ds(0, CHIPS - 1)], sem.plane_r.at[0])
    v.charge_sum[...] = added(v.charge_plane)
    stores[2].start()
    for store in stores:
        store.wait()


def output_kernel(*refs):
    count = len(OUTS)
    sem = refs[-1]
    copies = [pltpu.make_async_copy(refs[i], refs[count + i], sem.at[i]) for i in range(count)]
    for copy in copies:
        copy.start()
    for copy in copies:
        copy.wait()


def specs(space, count):
    return [pl.BlockSpec(memory_space=space)] * count


def body(
    positions, features, charge_weight, counts, mol_ids, energy_cot,
    lattice, filter_in, filter_mid, filter_out,
):
    shape = jax.ShapeDtypeStruct
    dma = pltpu.SemaphoreType.DMA
    signs = jnp.asarray(sign_matrix(), BF16)
    signs_t = jnp.asarray(sign_matrix().T, BF16)
    outs = tuple(shape(*out) for out in OUTS)
    sums = pl.pallas_call(
        whole_kernel,
        out_shape=outs,
        in_specs=specs(pltpu.SMEM, 1) + specs(pl.ANY, 11),
        out_specs=tuple(specs(pl.ANY, len(OUTS))),
        scratch_shapes=[pltpu.VMEM(dims, kind) for dims, kind in SCRATCH.values()]
        + [dma((count,)) for count in SEMAPHORES.values()],
        compiler_params=pltpu.CompilerParams(
            collective_id=0, has_side_effects=True, vmem_limit_bytes=56 * MIB
        ),
        name="ewald",
    )(
        counts, positions, features, charge_weight.T, mol_ids, energy_cot.reshape(1, MOLS), lattice,
        filter_in, filter_mid, filter_out.T, signs, signs_t,
    )
    mol, pos, charge, first, middle, last = pl.pallas_call(
        output_kernel,
        out_shape=outs,
        in_specs=specs(pltpu.VMEM, len(OUTS)),
        out_specs=tuple(specs(pl.ANY, len(OUTS))),
        scratch_shapes=[dma((len(OUTS),))],
        compiler_params=pltpu.CompilerParams(vmem_limit_bytes=56 * MIB),
        name="outputs",
    )(*sums)
    return (mol.reshape(MOLS), pos, charge.T, first, middle, last.T)


def solution(mesh):
    return jax.shard_map(
        body,
        mesh=mesh,
        in_specs=(
            P(None, "atoms"), P("atoms", None), P(), P("atoms"), P("atoms", None), P("atoms"),
            P(None, "kvec"), P(), P(), P(),
        ),
        out_specs=(P("atoms"), P(None, ("atoms", "kvec")), P(), P(), P(), P()),
        check_vma=False,
    )
```

```python
import functools
import math

import jax
import jax.numpy as jnp
import numpy as np
from jax import lax
from jax.experimental import pallas as pl
from jax.experimental.pallas import tpu as pltpu
from jax.sharding import PartitionSpec as P

MAXN = 12
BOX_EDGE = 40.0
MESH = pl.DeviceIdType.MESH
F32 = jnp.float32
BF16 = jnp.bfloat16

PLANE = 32
RING = 8
CAP = 4096
CH = 32
HID = 256
MOLS = 256
YZ = 640
XC = 256
HALF = 320
TILE = 512
TILES = CAP // TILE
CHIPS = 16
PAIR_ROWS = 80
BIG = 48
SMALL = 32
TABLE = 512
FAR_FIRST = (4, 3, 5, 2, 6, 1, 7)
CHIP_STEPS = sorted(
    ((dx, dy) for dx in range(4) for dy in range(4) if dx or dy),
    key=lambda step: -(min(step[0], 4 - step[0]) + min(step[1], 4 - step[1])),
)
MIB = 1 << 20


def row_of(y_index, z_index):
    if y_index is None and z_index is None:
        return 624
    if y_index is None:
        return 576 + z_index
    if z_index is None:
        return 600 + y_index
    return 24 * y_index + z_index


def half_plane():
    vectors = [(0, n3) for n3 in range(13)]
    return vectors + [(n2, n3) for n2 in range(1, 13) for n3 in range(-12, 13)]


def sign_matrix():
    def cosine(n):
        return None if n == 0 else n - 1

    def sine(n):
        return 12 + n - 1

    matrix = np.zeros((2 * HALF, YZ), np.float32)
    for index, (n2, n3) in enumerate(half_plane()):
        size, sign = abs(n3), (1.0 if n3 >= 0 else -1.0)
        matrix[index, row_of(cosine(n2), cosine(size))] = 1.0
        if n2 and size:
            matrix[index, row_of(sine(n2), sine(size))] = -sign
        if n2:
            matrix[HALF + index, row_of(sine(n2), cosine(size))] = 1.0
        if size:
            matrix[HALF + index, row_of(cosine(n2), sine(size))] = sign
    return matrix


def nt(first, second):
    return lax.dot_general(first, second, (((1,), (1,)), ((), ())), preferred_element_type=F32)


def tn(first, second):
    return lax.dot_general(first, second, (((0,), (0,)), ((), ())), preferred_element_type=F32)


def nn(first, second):
    return jnp.dot(first, second, preferred_element_type=F32)


def cos_turns(turns):
    frac = turns - jnp.floor(turns + 0.5)
    x = (2.0 * math.pi) * (0.25 - jnp.abs(frac))
    s = x * x
    poly = jnp.full_like(s, -1.0 / 39916800.0)
    for coefficient in (1.0 / 362880.0, -1.0 / 5040.0, 1.0 / 120.0, -1.0 / 6.0, 1.0):
        poly = poly * s + coefficient
    return x * poly


def rows_of_parts(value):
    high = value.astype(BF16).astype(F32)
    rest = value - high
    middle = rest.astype(BF16).astype(F32)
    low = rest - middle
    row = lax.broadcasted_iota(jnp.int32, (16, value.shape[1]), 0)
    parts = jnp.where(row == 0, high, jnp.where(row == 1, middle, jnp.where(row == 2, low, 0.0)))
    return parts.astype(BF16)


def yz_turns(coord):
    row = lax.broadcasted_iota(jnp.int32, (24, 1), 0)
    harmonic = jnp.where(row < 12, row + 1, row - 11).astype(F32)
    shift = jnp.where(row < 12, 0.0, 0.25)
    return harmonic * coord - shift, harmonic


def x_turns(coord, rank):
    row = lax.broadcasted_iota(jnp.int32, (8, 1), 0)
    harmonic = (2 * rank + lax.rem(row, 2)).astype(F32)
    shift = jnp.where(row < 2, 0.0, 0.25)
    return harmonic * coord - shift, harmonic


def lane_roll(value, shift):
    return pltpu.roll(value, shift % value.shape[1], 1)


def slope(preact, sigmoid_val):
    return sigmoid_val * (1.0 + preact * (1.0 - sigmoid_val))


def point_squares(rank, axis):
    dims = (2 * HALF, 1) if axis == 0 else (1, 2 * HALF)
    index = lax.broadcasted_iota(jnp.int32, dims, axis)
    n1 = (2 * rank + jnp.where(index >= HALF, 1, 0)).astype(F32)
    index = jnp.where(index >= HALF, index - HALF, index)
    later = (index - 13).astype(F32)
    n2 = jnp.where(index < 13, 0.0, 1.0 + jnp.floor((later + 0.5) * (1.0 / 25.0)))
    n3 = jnp.where(index < 13, index.astype(F32), later - 25.0 * (n2 - 1.0) - 12.0)
    return n1 * n1 + n2 * n2 + n3 * n3


def loop(low, high, action):
    def run(i, carry):
        action(i)
        return carry

    lax.fori_loop(low, high, run, 0)


def half_tiles(half):
    return [pl.ds(tile * TILE, TILE) for tile in range(half * TILES // 2, (half + 1) * TILES // 2)]


def functions(rank, v, half):
    for at in half_tiles(half):
        turns2, _ = yz_turns(v.pos[1:2, at])
        turns3, _ = yz_turns(v.pos[2:3, at])
        turns1, _ = x_turns(v.pos[0:1, at], rank)
        v.u2[:, at] = cos_turns(turns2)
        v.u3[:, at] = cos_turns(turns3)
        v.u1[:, at] = cos_turns(turns1)
        u3 = v.u3[:, at]
        for two in range(12):
            first = v.u2[2 * two : 2 * two + 1, at] * u3
            second = v.u2[2 * two + 1 : 2 * two + 2, at] * u3
            rows = jnp.concatenate([first, second], axis=0).astype(BF16)
            v.b[48 * two : 48 * two + 48, at] = rows
        v.b[576:624, at] = jnp.concatenate([u3, v.u2[:, at]], axis=0).astype(BF16)
        row = lax.broadcasted_iota(jnp.int32, (16, TILE), 0)
        v.b[624:640, at] = jnp.where(row == 0, 1.0, 0.0).astype(BF16)


def charges(count, v, half):
    cot_parts = rows_of_parts(v.cot[...])
    for at in half_tiles(half):
        slot = at.start + lax.broadcasted_iota(jnp.int32, (1, TILE), 1)
        alive = jnp.where(slot < count, 1.0, 0.0)
        v.alive[:, at] = alive
        molecule = lax.broadcasted_iota(jnp.int32, (MOLS, TILE), 0)
        member = jnp.where(molecule == v.ids[:, at], 1.0, 0.0).astype(BF16)
        v.member[:, at] = member
        weight = jnp.sum(nn(cot_parts, member), axis=0, keepdims=True)
        v.weight[:, at] = weight
        charge = (nt(v.cw[...], v.feat[at, :]) * alive).astype(BF16).astype(F32)
        pair = jnp.concatenate([charge, weight * charge], axis=0).astype(BF16)
        v.pair[:, at] = pair
        pair = pair.astype(F32)
        for j in range(4):
            v.a[64 * j : 64 * j + 64, at] = (v.u1[j : j + 1, at] * pair).astype(BF16)


def derivatives(rank, v):
    for half in range(2):
        for at in half_tiles(half):
            turns1, h1 = x_turns(v.pos[0:1, at], rank)
            turns2, h2 = yz_turns(v.pos[1:2, at])
            turns3, h3 = yz_turns(v.pos[2:3, at])
            v.d1[:, at] = h1 * cos_turns(turns1 + 0.25)
            v.d2[:, at] = h2 * cos_turns(turns2 + 0.25)
            v.d3[:, at] = h3 * cos_turns(turns3 + 0.25)


def structure_sum(v, rows, half):
    at = pl.ds(half * CAP // 2, CAP // 2)
    return nt(v.b[rows, at], v.a[:, at])


def network(squared, v):
    inverse = jnp.where(squared > 0.0, 1.0, 0.0) / (
        jnp.maximum(squared, 1.0) * math.sqrt(CAP * PLANE)
    )
    spacing = MAXN * math.sqrt(3.0) / 16
    center = (lax.broadcasted_iota(jnp.int32, (1, 16), 1).astype(F32) + 0.5) * spacing
    away = (jnp.sqrt(squared) - center) / spacing
    radial = jnp.exp(-0.5 * away * away).astype(BF16)
    pre_one = nn(radial, v.fin[...])
    sig_one = jax.nn.sigmoid(pre_one)
    act_one = (pre_one * sig_one).astype(BF16)
    pre_two = nn(act_one, v.fmid[...])
    sig_two = jax.nn.sigmoid(pre_two)
    act_two = (pre_two * sig_two).astype(BF16)
    logits = nn(act_two, v.fout_wide[...])
    return inverse, radial, pre_one, sig_one, act_one, pre_two, sig_two, act_two, logits


def filter_forward(rank, v):
    lane = lax.broadcasted_iota(jnp.int32, (CH, 128), 1)
    channel = lax.broadcasted_iota(jnp.int32, (CH, 128), 0)
    spread = jnp.where(lax.rem(lane, CH) == channel, 1.0, 0.0).astype(BF16)
    v.fout_wide[...] = tn(v.fout[...], spread).astype(BF16)
    values = network(point_squares(rank, 0), v)
    inverse, logits = values[0], values[-1]
    soft = jnp.maximum(logits, 0.0) + jnp.log1p(jnp.exp(-jnp.abs(logits)))
    soft = soft * inverse
    half_lane = lax.broadcasted_iota(jnp.int32, (HALF, 128), 1)
    v.filters[...] = jnp.where(half_lane < 64, soft[:HALF], soft[HALF:])


def table_forward(rank, v):
    table = lax.broadcasted_iota(jnp.int32, (TABLE, 1), 0).astype(F32)
    inverse, radial, pre_one, sig_one, act_one, pre_two, sig_two, act_two, logits = network(table, v)
    v.radial[...] = radial
    v.act_one[...] = act_one
    v.act_two[...] = act_two
    v.slope_one[...] = slope(pre_one, sig_one)
    v.slope_two[...] = slope(pre_two, sig_two)
    v.sigmoid[...] = jax.nn.sigmoid(logits) * inverse
    v.same[...] = jnp.where(table == point_squares(rank, 1), 1.0, 0.0).astype(BF16)


def multiplicities(rank, v):
    def chunk(index, total):
        k = v.lattice[index]
        k1, k2, k3 = k[0:1, :], k[1:2, :], k[2:3, :]
        back = k1 < 0
        k1 = jnp.where(back, -k1, k1)
        k2 = jnp.where(back, -k2, k2)
        k3 = jnp.where(back, -k3, k3)
        flip = (k2 < 0) | ((k2 == 0) & (k3 < 0))
        k2 = jnp.where(flip, -k2, k2)
        k3 = jnp.where(flip, -k3, k3)
        code = jnp.where(k2 == 0, k3, k2 * 25 + k3)
        width = k.shape[1]
        hit = lax.broadcasted_iota(jnp.int32, (HALF, width), 0) == code
        hit = jnp.where(hit, 1.0, 0.0).astype(BF16)
        row = lax.broadcasted_iota(jnp.int32, (16, width), 0)
        own = (k1 - 2 * rank) == lax.rem(row, 2)
        sign = jnp.where((row >= 2) & flip, -1.0, 1.0)
        select = jnp.where(own & (row < 4), sign, 0.0).astype(BF16)
        return total + nt(hit, select)

    counted = lax.fori_loop(0, RING, chunk, jnp.zeros((HALF, 16), F32))
    lane = lax.broadcasted_iota(jnp.int32, (HALF, 128), 1)
    v.both[...] = jnp.where(lane < 64, counted[:, 0:1], counted[:, 1:2])
    v.difference[...] = jnp.where(lane < 64, counted[:, 2:3], counted[:, 3:4])


def coefficients(v):
    signs = v.signs[...]
    total = jnp.concatenate(
        [
            jnp.concatenate([v.total[start : start + HALF], v.total[start + HALF : start + YZ]], axis=1)
            for start in (0, YZ)
        ],
        axis=0,
    )
    v.sums[...] = nn(signs, total)
    ncc, ncs = v.sums[:HALF, :128], v.sums[HALF:, :128]
    nsc, nss = v.sums[:HALF, 128:], v.sums[HALF:, 128:]
    filters = v.filters[...]
    fp, fd = filters * v.both[...], filters * v.difference[...]
    gcc = (fp * ncc - fd * nss).astype(BF16)
    gss = (fp * nss - fd * ncc).astype(BF16)
    gsc = (fp * nsc + fd * ncs).astype(BF16)
    gcs = (fp * ncs + fd * nsc).astype(BF16)
    v.coef[:HALF, :128] = gcc
    v.coef[HALF:, :128] = gcs
    v.coef[:HALF, 128:] = gsc
    v.coef[HALF:, 128:] = gss
    v.gt[...] = tn(v.coef[...], signs).astype(BF16)


def swapped_coefficients(v):
    g = nn(v.signs_t[...], v.coef[...])
    lane = lax.broadcasted_iota(jnp.int32, (YZ, XC), 1)
    swapped = jnp.where(lax.rem(lane, 64) < 32, lane_roll(g, -32), lane_roll(g, 32))
    v.gs[...] = swapped.astype(BF16)


def upstream_table(v):
    ncc, ncs = v.sums[:HALF, :128], v.sums[HALF:, :128]
    nsc, nss = v.sums[:HALF, 128:], v.sums[HALF:, 128:]
    tcc, tcs = lane_roll(ncc, -32), lane_roll(ncs, -32)
    tsc, tss = lane_roll(nsc, -32), lane_roll(nss, -32)
    upstream = 0.5 * (
        v.both[...] * (ncc * tcc + nss * tss + nsc * tsc + ncs * tcs)
        + v.difference[...] * (nsc * tcs + ncs * tsc - ncc * tss - nss * tcc)
    )
    upstream = jnp.concatenate([upstream, lane_roll(upstream, -64)], axis=0)
    lane = lax.broadcasted_iota(jnp.int32, (2 * HALF, 128), 1)
    upstream = jnp.where(lane < CH, upstream, 0.0)
    total = nn(v.same[0:128, :], upstream.astype(BF16))
    for group in range(1, 4):
        rows = v.same[128 * group : 128 * group + 128, :]
        total = total + nn(rows, lane_roll(upstream, 32 * group).astype(BF16))
    return total.astype(BF16)


def filter_backward(v):
    upstream = v.up_total[...].astype(F32)
    upstream = jnp.concatenate(
        [upstream] + [lane_roll(upstream, -32 * group) for group in range(1, 4)], axis=0
    )
    lane = lax.broadcasted_iota(jnp.int32, (TABLE, 128), 1)
    grad_logits = jnp.where(lane < CH, upstream * v.sigmoid[...], 0.0).astype(BF16)
    out_grad = tn(grad_logits, v.act_two[...])
    grad_two = (nt(grad_logits, v.fout_wide[...]) * v.slope_two[...]).astype(BF16)
    mid_grad = tn(v.act_one[...], grad_two)
    grad_one = (nt(grad_two, v.fmid[...]) * v.slope_one[...]).astype(BF16)
    return tn(v.radial[...], grad_one), mid_grad, out_grad[:CH]


GRAD_SCALE = 0.5 * 2.0 * math.pi / BOX_EDGE


def potential_pass(v):
    for tile in range(TILES):
        at = pl.ds(tile * TILE, TILE)
        u1 = v.u1[:, at]
        w = nn(v.gt[...], v.b[:, at])
        v.w[:, at] = w
        pot = sum(u1[j : j + 1, :] * w[64 * j : 64 * j + 64, :] for j in range(4))
        volt, other = pot[:CH], pot[CH:]
        v.volt[:, at] = volt
        v.cot_rows[:, at] = (0.5 * (v.weight[:, at] * volt + other) * v.alive[:, at]).astype(BF16)
    return nn(v.cot_rows[...], v.feat[...])


def molecule_sums(v):
    return jnp.sum(nt(rows_of_parts(v.energy[...]), v.member[...]), axis=0, keepdims=True)


def force_pass(v):
    def fold(value):
        return value[0:8] + value[8:16] + value[16:24]

    for tile in range(TILES):
        at = pl.ds(tile * TILE, TILE)
        v.response[:, at] = nn(v.gs[...], v.a[:, at])
        pair = v.pair[:, at].astype(F32)
        charge, weighted = pair[:CH], pair[CH:]
        v.energy[:, at] = 0.5 * jnp.sum(charge * v.volt[:, at], axis=0, keepdims=True)
        potx = sum(v.d1[j : j + 1, at] * v.w[64 * j : 64 * j + 64, at] for j in range(4))
        grad_x = jnp.sum(weighted * potx[:CH] + charge * potx[CH:], axis=0, keepdims=True)
        u3, d3 = v.u3[:, at], v.d3[:, at]
        sum_y = fold(v.d2[:, at] * v.response[600:624, at])
        sum_z = fold(d3 * v.response[576:600, at])
        for y in range(24):
            response = v.response[24 * y : 24 * y + 24, at]
            sum_y = sum_y + v.d2[y : y + 1, at] * fold(u3 * response)
            sum_z = sum_z + v.u2[y : y + 1, at] * fold(d3 * response)
        v.message[tile, 0:1, :] = grad_x * GRAD_SCALE
        v.message[tile, 1:2, :] = jnp.sum(sum_y, axis=0, keepdims=True) * GRAD_SCALE
        v.message[tile, 2:3, :] = jnp.sum(sum_z, axis=0, keepdims=True) * GRAD_SCALE


SCRATCH = dict(
    pos=((3, CAP), F32), feat=((CAP, 128), BF16), cw=((CH, 128), BF16), ids=((1, CAP), jnp.int32),
    cot=((1, MOLS), F32), fin=((16, HID), BF16), fmid=((HID, HID), BF16), fout=((CH, HID), BF16),
    signs=((2 * HALF, YZ), BF16), signs_t=((YZ, 2 * HALF), BF16), lattice=((RING, 3, 1024), jnp.int32),
    u1=((8, CAP), F32), u2=((24, CAP), F32), u3=((24, CAP), F32), d1=((8, CAP), F32), d2=((24, CAP), F32), d3=((24, CAP), F32),
    w=((XC, CAP), F32), volt=((CH, CAP), F32),
    alive=((1, CAP), F32), weight=((1, CAP), F32), member=((MOLS, CAP), BF16),
    pair=((2 * CH, CAP), BF16), b=((YZ, CAP), BF16), a=((XC, CAP), BF16), acc=((YZ, XC), F32),
    part=((YZ, 128), BF16), mate=((YZ, 128), BF16), half=((YZ, 128), BF16),
    inbox=((CHIPS, BIG, 128), BF16), total=((2 * YZ, 128), BF16),
    radial=((TABLE, 16), BF16), act_one=((TABLE, HID), BF16), act_two=((TABLE, HID), BF16),
    slope_one=((TABLE, HID), F32), slope_two=((TABLE, HID), F32), fout_wide=((HID, 128), BF16),
    sigmoid=((TABLE, 128), F32), same=((TABLE, 2 * HALF), BF16), filters=((HALF, 128), F32),
    both=((HALF, 128), F32), difference=((HALF, 128), F32),
    sums=((2 * HALF, XC), F32), coef=((2 * HALF, XC), BF16), energy=((1, CAP), F32), cot_rows=((CH, CAP), BF16),
    gt=((XC, YZ), BF16), gs=((YZ, XC), BF16), response=((YZ, CAP), F32),
    up=((128, 128), BF16), up_ring=((RING, 64, 128), BF16), up_total=((128, 128), BF16),
    message=((RING, 4, TILE), F32), message_box=((RING, 4, TILE), F32),
    charge_ring=((RING, CH, 128), BF16), charge_mine=((CH, 128), BF16), charge_mate=((CH, 128), BF16),
    charge_plane=((CHIPS, CH, 128), BF16),
)
SEMAPHORES = dict(
    load=11, mate_s=4, mate_r=4, scatter_s=1, scatter_r=1, gather_s=1, gather_r=1,
    ring_s=4, ring_r=4, plane_s=1, plane_r=1,
)
OUTS = (
    ((1, MOLS), F32), ((3, TILE), F32), ((CH, 128), F32), ((16, HID), F32), ((HID, HID), F32), ((CH, HID), F32),
)


class Names:
    def __init__(self, names, refs):
        for name, ref in zip(names, refs, strict=True):
            setattr(self, name, ref)


def whole_kernel(
    count_ref, pos_ref, feat_ref, cw_ref, ids_ref, cot_ref, lattice_ref, fin_ref, fmid_ref, fout_ref,
    signs_ref, signs_t_ref, mol_out, pos_out, charge_out, in_out, mid_out, out_out, *scratch,
):
    v = Names(SCRATCH, scratch[: len(SCRATCH)])
    sem = Names(SEMAPHORES, scratch[len(SCRATCH) :])
    plane, ring = lax.axis_index("atoms"), lax.axis_index("kvec")
    chip, core = plane // 2, lax.rem(plane, 2)
    rank = ring

    loads = [
        pltpu.make_async_copy(src, dst, sem.load.at[i])
        for i, (src, dst) in enumerate((
            (pos_ref, v.pos), (feat_ref, v.feat), (cw_ref, v.cw), (ids_ref, v.ids), (cot_ref, v.cot),
            (lattice_ref, v.lattice.at[ring]), (fin_ref, v.fin), (fmid_ref, v.fmid), (fout_ref, v.fout),
            (signs_ref, v.signs), (signs_t_ref, v.signs_t),
        ))
    ]
    for load in loads:
        load.start()
    def remote(src, dst, send, recv, device):
        return pltpu.make_async_remote_copy(
            src_ref=src, dst_ref=dst, send_sem=send, recv_sem=recv,
            device_id=device, device_id_type=MESH,
        )

    def await_bytes(ref, semaphore):
        pltpu.make_async_copy(ref, ref, semaphore).wait()

    def ring_peer(i):
        return (plane, lax.rem(ring + i, RING))

    def chip_device(which):
        return (2 * which + core, ring)

    def chip_at(step):
        return 4 * lax.rem(chip // 4 + step[0], 4) + lax.rem(lax.rem(chip, 4) + step[1], 4)

    mate = (plane + 1 - 2 * core, ring)

    barrier = pltpu.get_barrier_semaphore()

    def greet(device):
        pl.semaphore_signal(barrier, inc=1, device_id=device, device_id_type=MESH)

    loop(1, CHIPS, lambda i: greet(chip_device(lax.rem(chip + i, CHIPS))))
    loop(1, RING, lambda i: greet(ring_peer(i)))
    greet(mate)

    loads[0].wait()
    functions(rank, v, 0)
    for load in loads[1:5]:
        load.wait()
    charges(count_ref[0], v, 0)
    v.acc[...] = structure_sum(v, pl.ds(0, YZ), 0)
    functions(rank, v, 1)
    charges(count_ref[0], v, 1)

    def share(slots, phase):
        for i in FAR_FIRST:
            remote(slots.at[ring], slots.at[ring], sem.ring_s.at[phase], sem.ring_r.at[phase], ring_peer(i)).start()

    def shared(slots, phase):
        await_bytes(slots.at[pl.ds(0, RING - 1)], sem.ring_r.at[phase])

    def half_rows(which):
        return pl.ds(pl.multiple_of(YZ * which, YZ), YZ)

    def to_mate(src, dst, phase):
        return remote(src, dst, sem.mate_s.at[phase], sem.mate_r.at[phase], mate)

    def row_sums(which):
        rows = pl.ds(pl.multiple_of(HALF * which, HALF), HALF)
        return v.acc[rows, :] + structure_sum(v, rows, 1)

    theirs = row_sums(1 - core)
    v.part[:HALF, :] = theirs[:, :128].astype(BF16)
    v.part[HALF:, :] = theirs[:, 128:].astype(BF16)
    pl.semaphore_wait(barrier, CHIPS + RING - 1)
    swap_parts = to_mate(v.part, v.mate, 0)
    swap_parts.start()
    for load in loads[5:]:
        load.wait()
    share(v.lattice, 0)
    mine = row_sums(core)
    swap_parts.wait_recv()
    v.half[:HALF, :] = (mine[:, :128] + v.mate[:HALF, :].astype(F32)).astype(BF16)
    v.half[HALF:, :] = (mine[:, 128:] + v.mate[HALF:, :].astype(F32)).astype(BF16)

    def pair_rows(which, odd, base=0):
        start = base + PAIR_ROWS * which + (BIG if odd else 0)
        return pl.ds(pl.multiple_of(start, 16), SMALL if odd else BIG)

    my_pair, my_odd = chip // 2, lax.rem(chip, 2)

    def scatter(odd):
        for step in CHIP_STEPS:
            other = chip_at(step)
            other_odd = (odd + step[1]) % 2
            size = SMALL if other_odd else BIG
            remote(
                v.half.at[pair_rows(other // 2, other_odd)], v.inbox.at[chip, pl.ds(0, size)],
                sem.scatter_s.at[0], sem.scatter_r.at[0], chip_device(other),
            ).start()

    pl.when(my_odd == 0)(lambda: scatter(0))
    pl.when(my_odd == 1)(lambda: scatter(1))
    derivatives(rank, v)
    filter_forward(rank, v)
    table_forward(rank, v)

    def reduce(odd):
        size = SMALL if odd else BIG
        v.inbox[chip, :size] = v.half[pair_rows(my_pair, odd)]
        await_bytes(v.inbox.at[pl.ds(0, CHIPS - 1), pl.ds(0, size)], sem.scatter_r.at[0])
        value = v.inbox[0, :size].astype(F32)
        for slot in range(1, CHIPS):
            value = value + v.inbox[slot, :size].astype(F32)
        rows = pair_rows(my_pair, odd, YZ * core)
        v.total[rows] = value.astype(BF16)

        for step in CHIP_STEPS:
            remote(
                v.total.at[rows], v.total.at[rows], sem.gather_s.at[0], sem.gather_r.at[0],
                chip_device(chip_at(step)),
            ).start()

    pl.when(my_odd == 0)(lambda: reduce(0))
    pl.when(my_odd == 1)(lambda: reduce(1))

    shared(v.lattice, 0)
    multiplicities(rank, v)

    def reduced(odd):
        size = SMALL if odd else BIG
        await_bytes(v.total.at[pl.ds(0, YZ - size)], sem.gather_r.at[0])
        await_bytes(v.total.at[pl.ds(0, YZ - size)], sem.scatter_s.at[0])

    pl.when(my_odd == 0)(lambda: reduced(0))
    pl.when(my_odd == 1)(lambda: reduced(1))
    swap_totals = to_mate(v.total.at[half_rows(core)], v.total.at[half_rows(core)], 1)
    swap_totals.start()
    swap_totals.wait_recv()

    coefficients(v)
    v.charge_ring[ring] = potential_pass(v).astype(BF16)
    share(v.charge_ring, 2)
    v.up[...] = upstream_table(v)
    up_rows = pl.ds(pl.multiple_of(64 * core, 64), 64)
    v.up_ring[ring] = v.up[up_rows, :]
    share(v.up_ring, 1)

    swapped_coefficients(v)
    force_pass(v)
    molecules = molecule_sums(v)
    for chunk in range(RING):
        v.message[chunk, 3:4, 0:MOLS] = molecules
        v.message[chunk, 3:4, MOLS:TILE] = jnp.zeros((1, TILE - MOLS), F32)
    for i in FAR_FIRST:
        peer = lax.rem(ring + i, RING)
        remote(v.message.at[peer], v.message_box.at[ring], sem.ring_s.at[3], sem.ring_r.at[3], ring_peer(i)).start()
    v.message_box[ring] = v.message[ring]

    def added(slots):
        value = slots[0].astype(F32)
        for slot in range(1, slots.shape[0]):
            value = value + slots[slot].astype(F32)
        return value

    shared(v.charge_ring, 2)
    v.charge_mine[...] = added(v.charge_ring).astype(BF16)
    swap_charge = to_mate(v.charge_mine, v.charge_mate, 3)
    swap_charge.start()
    swap_charge.wait_recv()
    v.charge_plane[chip] = (v.charge_mine[...].astype(F32) + v.charge_mate[...].astype(F32)).astype(BF16)
    for step in CHIP_STEPS:
        remote(
            v.charge_plane.at[chip], v.charge_plane.at[chip], sem.plane_s.at[0], sem.plane_r.at[0],
            chip_device(chip_at(step)),
        ).start()

    shared(v.up_ring, 1)
    v.up_total[up_rows, :] = added(v.up_ring).astype(BF16)
    swap_up = to_mate(v.up_total.at[up_rows], v.up_total.at[up_rows], 2)
    swap_up.start()
    swap_up.wait_recv()
    in_out[...], mid_out[...], out_out[...] = filter_backward(v)
    shared(v.message_box, 3)
    value = added(v.message_box)
    pos_out[...] = value[0:3]
    mol_out[...] = value[3:4, :MOLS]

    for swap in (swap_parts, swap_totals, swap_up, swap_charge):
        swap.wait_send()
    for phase, slots in enumerate((v.lattice, v.up_ring, v.charge_ring, v.message)):
        await_bytes(slots.at[pl.ds(0, RING - 1)], sem.ring_s.at[phase])

    def gathered(odd):
        size = SMALL if odd else BIG
        await_bytes(v.inbox.at[pl.ds(0, CHIPS - 1), pl.ds(0, size)], sem.gather_s.at[0])

    pl.when(my_odd == 0)(lambda: gathered(0))
    pl.when(my_odd == 1)(lambda: gathered(1))
    await_bytes(v.charge_plane.at[pl.ds(0, CHIPS - 1)], sem.plane_s.at[0])

    await_bytes(v.charge_plane.at[pl.ds(0, CHIPS - 1)], sem.plane_r.at[0])
    charge_out[...] = added(v.charge_plane)


def output_kernel(*refs):
    count = len(OUTS)
    sem = refs[-1]
    copies = [pltpu.make_async_copy(refs[i], refs[count + i], sem.at[i]) for i in range(count)]
    for copy in copies:
        copy.start()
    for copy in copies:
        copy.wait()


def specs(space, count):
    return [pl.BlockSpec(memory_space=space)] * count


def body(
    positions, features, charge_weight, counts, mol_ids, energy_cot,
    lattice, filter_in, filter_mid, filter_out,
):
    shape = jax.ShapeDtypeStruct
    dma = pltpu.SemaphoreType.DMA
    signs = jnp.asarray(sign_matrix(), BF16)
    signs_t = jnp.asarray(sign_matrix().T, BF16)
    outs = tuple(shape(*out) for out in OUTS)
    sums = pl.pallas_call(
        whole_kernel,
        out_shape=tuple(pltpu.VMEM(*out) for out in OUTS),
        in_specs=specs(pltpu.SMEM, 1) + specs(pl.ANY, 11),
        out_specs=tuple(specs(pltpu.VMEM, len(OUTS))),
        scratch_shapes=[pltpu.VMEM(dims, kind) for dims, kind in SCRATCH.values()]
        + [dma((count,)) for count in SEMAPHORES.values()],
        compiler_params=pltpu.CompilerParams(
            collective_id=0, has_side_effects=True, vmem_limit_bytes=56 * MIB
        ),
        name="ewald",
    )(
        counts, positions, features, charge_weight.T, mol_ids, energy_cot.reshape(1, MOLS), lattice,
        filter_in, filter_mid, filter_out.T, signs, signs_t,
    )
    mol, pos, charge, first, middle, last = pl.pallas_call(
        output_kernel,
        out_shape=outs,
        in_specs=specs(pltpu.VMEM, len(OUTS)),
        out_specs=tuple(specs(pl.ANY, len(OUTS))),
        scratch_shapes=[dma((len(OUTS),))],
        compiler_params=pltpu.CompilerParams(vmem_limit_bytes=56 * MIB),
        name="outputs",
    )(*[pltpu.with_memory_space_constraint(value, pltpu.VMEM) for value in sums])
    return (mol.reshape(MOLS), pos, charge.T, first, middle, last.T)


def solution(mesh):
    return jax.shard_map(
        body,
        mesh=mesh,
        in_specs=(
            P(None, "atoms"), P("atoms", None), P(), P("atoms"), P("atoms", None), P("atoms"),
            P(None, "kvec"), P(), P(), P(),
        ),
        out_specs=(P("atoms"), P(None, ("atoms", "kvec")), P(), P(), P(), P()),
        check_vma=False,
    )
```

```python
import functools
import math

import jax
import jax.numpy as jnp
import numpy as np
from jax import lax
from jax.experimental import pallas as pl
from jax.experimental.pallas import tpu as pltpu
from jax.sharding import PartitionSpec as P

MAXN = 12
BOX_EDGE = 40.0
MESH = pl.DeviceIdType.MESH
F32 = jnp.float32
BF16 = jnp.bfloat16

PLANE = 32
RING = 8
CAP = 4096
CH = 32
HID = 256
MOLS = 256
YZ = 640
XC = 256
HALF = 320
TILE = 512
TILES = CAP // TILE
CHIPS = 16
PAIR_ROWS = 80
BIG = 48
SMALL = 32
TABLE = 512
FAR_FIRST = (4, 3, 5, 2, 6, 1, 7)
CHIP_STEPS = sorted(
    ((dx, dy) for dx in range(4) for dy in range(4) if dx or dy),
    key=lambda step: -(min(step[0], 4 - step[0]) + min(step[1], 4 - step[1])),
)
MIB = 1 << 20


def row_of(y_index, z_index):
    if y_index is None and z_index is None:
        return 624
    if y_index is None:
        return 576 + z_index
    if z_index is None:
        return 600 + y_index
    return 24 * y_index + z_index


def half_plane():
    vectors = [(0, n3) for n3 in range(13)]
    return vectors + [(n2, n3) for n2 in range(1, 13) for n3 in range(-12, 13)]


def sign_matrix():
    def cosine(n):
        return None if n == 0 else n - 1

    def sine(n):
        return 12 + n - 1

    matrix = np.zeros((2 * HALF, YZ), np.float32)
    for index, (n2, n3) in enumerate(half_plane()):
        size, sign = abs(n3), (1.0 if n3 >= 0 else -1.0)
        matrix[index, row_of(cosine(n2), cosine(size))] = 1.0
        if n2 and size:
            matrix[index, row_of(sine(n2), sine(size))] = -sign
        if n2:
            matrix[HALF + index, row_of(sine(n2), cosine(size))] = 1.0
        if size:
            matrix[HALF + index, row_of(cosine(n2), sine(size))] = sign
    return matrix


def nt(first, second):
    return lax.dot_general(first, second, (((1,), (1,)), ((), ())), preferred_element_type=F32)


def tn(first, second):
    return lax.dot_general(first, second, (((0,), (0,)), ((), ())), preferred_element_type=F32)


def nn(first, second):
    return jnp.dot(first, second, preferred_element_type=F32)


def cos_turns(turns):
    frac = turns - jnp.floor(turns + 0.5)
    x = (2.0 * math.pi) * (0.25 - jnp.abs(frac))
    s = x * x
    poly = jnp.full_like(s, -1.0 / 39916800.0)
    for coefficient in (1.0 / 362880.0, -1.0 / 5040.0, 1.0 / 120.0, -1.0 / 6.0, 1.0):
        poly = poly * s + coefficient
    return x * poly


def rows_of_parts(value):
    high = value.astype(BF16).astype(F32)
    rest = value - high
    middle = rest.astype(BF16).astype(F32)
    low = rest - middle
    row = lax.broadcasted_iota(jnp.int32, (16, value.shape[1]), 0)
    parts = jnp.where(row == 0, high, jnp.where(row == 1, middle, jnp.where(row == 2, low, 0.0)))
    return parts.astype(BF16)


def yz_turns(coord):
    row = lax.broadcasted_iota(jnp.int32, (24, 1), 0)
    harmonic = jnp.where(row < 12, row + 1, row - 11).astype(F32)
    shift = jnp.where(row < 12, 0.0, 0.25)
    return harmonic * coord - shift, harmonic


def x_turns(coord, rank):
    row = lax.broadcasted_iota(jnp.int32, (8, 1), 0)
    harmonic = (2 * rank + lax.rem(row, 2)).astype(F32)
    shift = jnp.where(row < 2, 0.0, 0.25)
    return harmonic * coord - shift, harmonic


def lane_roll(value, shift):
    return pltpu.roll(value, shift % value.shape[1], 1)


def slope(preact, sigmoid_val):
    return sigmoid_val * (1.0 + preact * (1.0 - sigmoid_val))


def point_squares(rank, axis):
    dims = (2 * HALF, 1) if axis == 0 else (1, 2 * HALF)
    index = lax.broadcasted_iota(jnp.int32, dims, axis)
    n1 = (2 * rank + jnp.where(index >= HALF, 1, 0)).astype(F32)
    index = jnp.where(index >= HALF, index - HALF, index)
    later = (index - 13).astype(F32)
    n2 = jnp.where(index < 13, 0.0, 1.0 + jnp.floor((later + 0.5) * (1.0 / 25.0)))
    n3 = jnp.where(index < 13, index.astype(F32), later - 25.0 * (n2 - 1.0) - 12.0)
    return n1 * n1 + n2 * n2 + n3 * n3


def loop(low, high, action):
    def run(i, carry):
        action(i)
        return carry

    lax.fori_loop(low, high, run, 0)


def half_tiles(half):
    return [pl.ds(tile * TILE, TILE) for tile in range(half * TILES // 2, (half + 1) * TILES // 2)]


def functions(rank, v, half):
    for at in half_tiles(half):
        turns2, _ = yz_turns(v.pos[1:2, at])
        turns3, _ = yz_turns(v.pos[2:3, at])
        turns1, _ = x_turns(v.pos[0:1, at], rank)
        v.u2[:, at] = cos_turns(turns2)
        v.u3[:, at] = cos_turns(turns3)
        v.u1[:, at] = cos_turns(turns1)
        u3 = v.u3[:, at]
        for two in range(12):
            first = v.u2[2 * two : 2 * two + 1, at] * u3
            second = v.u2[2 * two + 1 : 2 * two + 2, at] * u3
            rows = jnp.concatenate([first, second], axis=0).astype(BF16)
            v.b[48 * two : 48 * two + 48, at] = rows
        v.b[576:624, at] = jnp.concatenate([u3, v.u2[:, at]], axis=0).astype(BF16)
        row = lax.broadcasted_iota(jnp.int32, (16, TILE), 0)
        v.b[624:640, at] = jnp.where(row == 0, 1.0, 0.0).astype(BF16)


def charges(count, v, half):
    cot_parts = rows_of_parts(v.cot[...])
    for at in half_tiles(half):
        slot = at.start + lax.broadcasted_iota(jnp.int32, (1, TILE), 1)
        alive = jnp.where(slot < count, 1.0, 0.0)
        v.alive[:, at] = alive
        molecule = lax.broadcasted_iota(jnp.int32, (MOLS, TILE), 0)
        member = jnp.where(molecule == v.ids[:, at], 1.0, 0.0).astype(BF16)
        v.member[:, at] = member
        weight = jnp.sum(nn(cot_parts, member), axis=0, keepdims=True)
        v.weight[:, at] = weight
        charge = (nt(v.cw[...], v.feat[at, :]) * alive).astype(BF16).astype(F32)
        pair = jnp.concatenate([charge, weight * charge], axis=0).astype(BF16)
        v.pair[:, at] = pair
        pair = pair.astype(F32)
        for j in range(4):
            v.a[64 * j : 64 * j + 64, at] = (v.u1[j : j + 1, at] * pair).astype(BF16)


def derivatives(rank, v):
    for half in range(2):
        for at in half_tiles(half):
            v.member_t[at, :] = v.member[:, at].T
            turns1, h1 = x_turns(v.pos[0:1, at], rank)
            turns2, h2 = yz_turns(v.pos[1:2, at])
            turns3, h3 = yz_turns(v.pos[2:3, at])
            v.d1[:, at] = h1 * cos_turns(turns1 + 0.25)
            v.d2[:, at] = h2 * cos_turns(turns2 + 0.25)
            v.d3[:, at] = h3 * cos_turns(turns3 + 0.25)


def structure_sum(v, rows, half):
    at = pl.ds(half * CAP // 2, CAP // 2)
    return nt(v.b[rows, at], v.a[:, at])


def network(squared, v):
    inverse = jnp.where(squared > 0.0, 1.0, 0.0) / (
        jnp.maximum(squared, 1.0) * math.sqrt(CAP * PLANE)
    )
    spacing = MAXN * math.sqrt(3.0) / 16
    center = (lax.broadcasted_iota(jnp.int32, (1, 16), 1).astype(F32) + 0.5) * spacing
    away = (jnp.sqrt(squared) - center) / spacing
    radial = jnp.exp(-0.5 * away * away).astype(BF16)
    pre_one = nn(radial, v.fin[...])
    sig_one = jax.nn.sigmoid(pre_one)
    act_one = (pre_one * sig_one).astype(BF16)
    pre_two = nn(act_one, v.fmid[...])
    sig_two = jax.nn.sigmoid(pre_two)
    act_two = (pre_two * sig_two).astype(BF16)
    logits = nn(act_two, v.fout_wide[...])
    return inverse, radial, pre_one, sig_one, act_one, pre_two, sig_two, act_two, logits


def filter_forward(rank, v):
    lane = lax.broadcasted_iota(jnp.int32, (CH, 128), 1)
    channel = lax.broadcasted_iota(jnp.int32, (CH, 128), 0)
    spread = jnp.where(lax.rem(lane, CH) == channel, 1.0, 0.0).astype(BF16)
    v.fout_wide[...] = tn(v.fout[...], spread).astype(BF16)
    values = network(point_squares(rank, 0), v)
    inverse, logits = values[0], values[-1]
    soft = jnp.maximum(logits, 0.0) + jnp.log1p(jnp.exp(-jnp.abs(logits)))
    soft = soft * inverse
    half_lane = lax.broadcasted_iota(jnp.int32, (HALF, 128), 1)
    v.filters[...] = jnp.where(half_lane < 64, soft[:HALF], soft[HALF:])


def table_forward(rank, v):
    table = lax.broadcasted_iota(jnp.int32, (TABLE, 1), 0).astype(F32)
    inverse, radial, pre_one, sig_one, act_one, pre_two, sig_two, act_two, logits = network(table, v)
    v.radial[...] = radial
    v.act_one[...] = act_one
    v.act_two[...] = act_two
    v.slope_one[...] = slope(pre_one, sig_one)
    v.slope_two[...] = slope(pre_two, sig_two)
    v.sigmoid[...] = jax.nn.sigmoid(logits) * inverse
    v.same[...] = jnp.where(table == point_squares(rank, 1), 1.0, 0.0).astype(BF16)


def multiplicities(rank, v):
    def chunk(index, total):
        k = v.lattice[index]
        k1, k2, k3 = k[0:1, :], k[1:2, :], k[2:3, :]
        back = k1 < 0
        k1 = jnp.where(back, -k1, k1)
        k2 = jnp.where(back, -k2, k2)
        k3 = jnp.where(back, -k3, k3)
        flip = (k2 < 0) | ((k2 == 0) & (k3 < 0))
        k2 = jnp.where(flip, -k2, k2)
        k3 = jnp.where(flip, -k3, k3)
        code = jnp.where(k2 == 0, k3, k2 * 25 + k3)
        width = k.shape[1]
        hit = lax.broadcasted_iota(jnp.int32, (HALF, width), 0) == code
        hit = jnp.where(hit, 1.0, 0.0).astype(BF16)
        row = lax.broadcasted_iota(jnp.int32, (16, width), 0)
        own = (k1 - 2 * rank) == lax.rem(row, 2)
        sign = jnp.where((row >= 2) & flip, -1.0, 1.0)
        select = jnp.where(own & (row < 4), sign, 0.0).astype(BF16)
        return total + nt(hit, select)

    counted = lax.fori_loop(0, RING, chunk, jnp.zeros((HALF, 16), F32))
    lane = lax.broadcasted_iota(jnp.int32, (HALF, 128), 1)
    v.both[...] = jnp.where(lane < 64, counted[:, 0:1], counted[:, 1:2])
    v.difference[...] = jnp.where(lane < 64, counted[:, 2:3], counted[:, 3:4])
    v.filter_both[...] = v.filters[...] * v.both[...]
    v.filter_difference[...] = v.filters[...] * v.difference[...]


def coefficients(v):
    signs = v.signs[...]
    total = jnp.concatenate(
        [
            jnp.concatenate([v.total[start : start + HALF], v.total[start + HALF : start + YZ]], axis=1)
            for start in (0, YZ)
        ],
        axis=0,
    )
    v.sums[...] = nn(signs, total)
    ncc, ncs = v.sums[:HALF, :128], v.sums[HALF:, :128]
    nsc, nss = v.sums[:HALF, 128:], v.sums[HALF:, 128:]
    fp, fd = v.filter_both[...], v.filter_difference[...]
    gcc = (fp * ncc - fd * nss).astype(BF16)
    gss = (fp * nss - fd * ncc).astype(BF16)
    gsc = (fp * nsc + fd * ncs).astype(BF16)
    gcs = (fp * ncs + fd * nsc).astype(BF16)
    v.coef[:HALF, :128] = gcc
    v.coef[HALF:, :128] = gcs
    v.coef[:HALF, 128:] = gsc
    v.coef[HALF:, 128:] = gss
    v.gt[...] = tn(v.coef[...], signs).astype(BF16)


def swapped_coefficients(v):
    g = nn(v.signs_t[...], v.coef[...])
    lane = lax.broadcasted_iota(jnp.int32, (YZ, XC), 1)
    swapped = jnp.where(lax.rem(lane, 64) < 32, lane_roll(g, -32), lane_roll(g, 32))
    v.gs[...] = swapped.astype(BF16)


def upstream_table(v):
    ncc, ncs = v.sums[:HALF, :128], v.sums[HALF:, :128]
    nsc, nss = v.sums[:HALF, 128:], v.sums[HALF:, 128:]
    tcc, tcs = lane_roll(ncc, -32), lane_roll(ncs, -32)
    tsc, tss = lane_roll(nsc, -32), lane_roll(nss, -32)
    upstream = 0.5 * (
        v.both[...] * (ncc * tcc + nss * tss + nsc * tsc + ncs * tcs)
        + v.difference[...] * (nsc * tcs + ncs * tsc - ncc * tss - nss * tcc)
    )
    upstream = jnp.concatenate([upstream, lane_roll(upstream, -64)], axis=0)
    lane = lax.broadcasted_iota(jnp.int32, (2 * HALF, 128), 1)
    upstream = jnp.where(lane < CH, upstream, 0.0)
    total = nn(v.same[0:128, :], upstream.astype(BF16))
    for group in range(1, 4):
        rows = v.same[128 * group : 128 * group + 128, :]
        total = total + nn(rows, lane_roll(upstream, 32 * group).astype(BF16))
    return total.astype(BF16)


def filter_backward(v):
    upstream = v.up_total[...].astype(F32)
    upstream = jnp.concatenate(
        [upstream] + [lane_roll(upstream, -32 * group) for group in range(1, 4)], axis=0
    )
    lane = lax.broadcasted_iota(jnp.int32, (TABLE, 128), 1)
    grad_logits = jnp.where(lane < CH, upstream * v.sigmoid[...], 0.0).astype(BF16)
    out_grad = tn(grad_logits, v.act_two[...])
    grad_two = (nt(grad_logits, v.fout_wide[...]) * v.slope_two[...]).astype(BF16)
    mid_grad = tn(v.act_one[...], grad_two)
    grad_one = (nt(grad_two, v.fmid[...]) * v.slope_one[...]).astype(BF16)
    return tn(v.radial[...], grad_one), mid_grad, out_grad[:CH]


GRAD_SCALE = 0.5 * 2.0 * math.pi / BOX_EDGE


def potential_pass(v):
    for tile in range(TILES):
        at = pl.ds(tile * TILE, TILE)
        u1 = v.u1[:, at]
        w = nn(v.gt[...], v.b[:, at])
        v.w[:, at] = w
        pot = sum(u1[j : j + 1, :] * w[64 * j : 64 * j + 64, :] for j in range(4))
        volt, other = pot[:CH], pot[CH:]
        v.volt[:, at] = volt
        v.cot_rows[:, at] = (0.5 * (v.weight[:, at] * volt + other) * v.alive[:, at]).astype(BF16)
    return nn(v.cot_rows[...], v.feat[...])


def molecule_sums(v):
    return jnp.sum(nn(rows_of_parts(v.energy[...]), v.member_t[...]), axis=0, keepdims=True)


def force_pass(v):
    def fold(value):
        return value[0:8] + value[8:16] + value[16:24]

    for tile in range(TILES):
        at = pl.ds(tile * TILE, TILE)
        v.response[:, at] = nn(v.gs[...], v.a[:, at])
        pair = v.pair[:, at].astype(F32)
        charge, weighted = pair[:CH], pair[CH:]
        v.energy[:, at] = 0.5 * jnp.sum(charge * v.volt[:, at], axis=0, keepdims=True)
        potx = sum(v.d1[j : j + 1, at] * v.w[64 * j : 64 * j + 64, at] for j in range(4))
        grad_x = jnp.sum(weighted * potx[:CH] + charge * potx[CH:], axis=0, keepdims=True)
        u3, d3 = v.u3[:, at], v.d3[:, at]
        sum_y = fold(v.d2[:, at] * v.response[600:624, at])
        sum_z = fold(d3 * v.response[576:600, at])
        for y in range(24):
            response = v.response[24 * y : 24 * y + 24, at]
            sum_y = sum_y + v.d2[y : y + 1, at] * fold(u3 * response)
            sum_z = sum_z + v.u2[y : y + 1, at] * fold(d3 * response)
        v.message[tile, 0:1, :] = grad_x * GRAD_SCALE
        v.message[tile, 1:2, :] = jnp.sum(sum_y, axis=0, keepdims=True) * GRAD_SCALE
        v.message[tile, 2:3, :] = jnp.sum(sum_z, axis=0, keepdims=True) * GRAD_SCALE


SCRATCH = dict(
    pos=((3, CAP), F32), feat=((CAP, 128), BF16), cw=((CH, 128), BF16), ids=((1, CAP), jnp.int32),
    cot=((1, MOLS), F32), fin=((16, HID), BF16), fmid=((HID, HID), BF16), fout=((CH, HID), BF16),
    signs=((2 * HALF, YZ), BF16), signs_t=((YZ, 2 * HALF), BF16), lattice=((RING, 3, 1024), jnp.int32),
    u1=((8, CAP), F32), u2=((24, CAP), F32), u3=((24, CAP), F32), d1=((8, CAP), F32), d2=((24, CAP), F32), d3=((24, CAP), F32),
    w=((XC, CAP), F32), volt=((CH, CAP), F32),
    alive=((1, CAP), F32), weight=((1, CAP), F32), member=((MOLS, CAP), BF16), member_t=((CAP, MOLS), BF16),
    pair=((2 * CH, CAP), BF16), b=((YZ, CAP), BF16), a=((XC, CAP), BF16), acc=((YZ, XC), F32),
    part=((YZ, 128), BF16), mate=((YZ, 128), BF16), half=((YZ, 128), BF16),
    inbox=((CHIPS, BIG, 128), BF16), total=((2 * YZ, 128), BF16),
    radial=((TABLE, 16), BF16), act_one=((TABLE, HID), BF16), act_two=((TABLE, HID), BF16),
    slope_one=((TABLE, HID), F32), slope_two=((TABLE, HID), F32), fout_wide=((HID, 128), BF16),
    sigmoid=((TABLE, 128), F32), same=((TABLE, 2 * HALF), BF16), filters=((HALF, 128), F32),
    both=((HALF, 128), F32), difference=((HALF, 128), F32),
    filter_both=((HALF, 128), F32), filter_difference=((HALF, 128), F32),
    sums=((2 * HALF, XC), F32), coef=((2 * HALF, XC), BF16), energy=((1, CAP), F32), cot_rows=((CH, CAP), BF16),
    gt=((XC, YZ), BF16), gs=((YZ, XC), BF16), response=((YZ, CAP), F32),
    up=((128, 128), BF16), up_ring=((RING, 64, 128), BF16), up_total=((128, 128), BF16),
    message=((RING, 4, TILE), F32), message_box=((RING, 4, TILE), F32),
    charge_ring=((RING, CH, 128), BF16), charge_mine=((CH, 128), BF16), charge_mate=((CH, 128), BF16),
    charge_plane=((CHIPS, CH, 128), BF16),
)
SEMAPHORES = dict(
    load=11, mate_s=4, mate_r=4, scatter_s=1, scatter_r=1, gather_s=1, gather_r=1,
    ring_s=4, ring_r=4, plane_s=1, plane_r=1,
)
OUTS = (
    ((1, MOLS), F32), ((3, TILE), F32), ((CH, 128), F32), ((16, HID), F32), ((HID, HID), F32), ((CH, HID), F32),
)


class Names:
    def __init__(self, names, refs):
        for name, ref in zip(names, refs, strict=True):
            setattr(self, name, ref)


def whole_kernel(
    count_ref, pos_ref, feat_ref, cw_ref, ids_ref, cot_ref, lattice_ref, fin_ref, fmid_ref, fout_ref,
    signs_ref, signs_t_ref, mol_out, pos_out, charge_out, in_out, mid_out, out_out, *scratch,
):
    v = Names(SCRATCH, scratch[: len(SCRATCH)])
    sem = Names(SEMAPHORES, scratch[len(SCRATCH) :])
    plane, ring = lax.axis_index("atoms"), lax.axis_index("kvec")
    chip, core = plane // 2, lax.rem(plane, 2)
    rank = ring

    loads = [
        pltpu.make_async_copy(src, dst, sem.load.at[i])
        for i, (src, dst) in enumerate((
            (pos_ref, v.pos), (feat_ref, v.feat), (cw_ref, v.cw), (ids_ref, v.ids), (cot_ref, v.cot),
            (lattice_ref, v.lattice.at[ring]), (fin_ref, v.fin), (fmid_ref, v.fmid), (fout_ref, v.fout),
            (signs_ref, v.signs), (signs_t_ref, v.signs_t),
        ))
    ]
    for load in loads:
        load.start()
    def remote(src, dst, send, recv, device):
        return pltpu.make_async_remote_copy(
            src_ref=src, dst_ref=dst, send_sem=send, recv_sem=recv,
            device_id=device, device_id_type=MESH,
        )

    def await_bytes(ref, semaphore):
        pltpu.make_async_copy(ref, ref, semaphore).wait()

    def ring_peer(i):
        return (plane, lax.rem(ring + i, RING))

    def chip_device(which):
        return (2 * which + core, ring)

    def chip_at(step):
        return 4 * lax.rem(chip // 4 + step[0], 4) + lax.rem(lax.rem(chip, 4) + step[1], 4)

    mate = (plane + 1 - 2 * core, ring)

    barrier = pltpu.get_barrier_semaphore()

    def greet(device):
        pl.semaphore_signal(barrier, inc=1, device_id=device, device_id_type=MESH)

    loop(1, CHIPS, lambda i: greet(chip_device(lax.rem(chip + i, CHIPS))))
    loop(1, RING, lambda i: greet(ring_peer(i)))
    greet(mate)

    loads[0].wait()
    functions(rank, v, 0)
    for load in loads[1:5]:
        load.wait()
    charges(count_ref[0], v, 0)
    v.acc[...] = structure_sum(v, pl.ds(0, YZ), 0)
    functions(rank, v, 1)
    charges(count_ref[0], v, 1)

    def share(slots, phase):
        for i in FAR_FIRST:
            remote(slots.at[ring], slots.at[ring], sem.ring_s.at[phase], sem.ring_r.at[phase], ring_peer(i)).start()

    def shared(slots, phase):
        await_bytes(slots.at[pl.ds(0, RING - 1)], sem.ring_r.at[phase])

    def half_rows(which):
        return pl.ds(pl.multiple_of(YZ * which, YZ), YZ)

    def to_mate(src, dst, phase):
        return remote(src, dst, sem.mate_s.at[phase], sem.mate_r.at[phase], mate)

    def row_sums(which):
        rows = pl.ds(pl.multiple_of(HALF * which, HALF), HALF)
        return v.acc[rows, :] + structure_sum(v, rows, 1)

    theirs = row_sums(1 - core)
    v.part[:HALF, :] = theirs[:, :128].astype(BF16)
    v.part[HALF:, :] = theirs[:, 128:].astype(BF16)
    pl.semaphore_wait(barrier, CHIPS + RING - 1)
    swap_parts = to_mate(v.part, v.mate, 0)
    swap_parts.start()
    for load in loads[5:]:
        load.wait()
    share(v.lattice, 0)
    mine = row_sums(core)
    swap_parts.wait_recv()
    v.half[:HALF, :] = (mine[:, :128] + v.mate[:HALF, :].astype(F32)).astype(BF16)
    v.half[HALF:, :] = (mine[:, 128:] + v.mate[HALF:, :].astype(F32)).astype(BF16)

    def pair_rows(which, odd, base=0):
        start = base + PAIR_ROWS * which + (BIG if odd else 0)
        return pl.ds(pl.multiple_of(start, 16), SMALL if odd else BIG)

    my_pair, my_odd = chip // 2, lax.rem(chip, 2)

    def scatter(odd):
        for step in CHIP_STEPS:
            other = chip_at(step)
            other_odd = (odd + step[1]) % 2
            size = SMALL if other_odd else BIG
            remote(
                v.half.at[pair_rows(other // 2, other_odd)], v.inbox.at[chip, pl.ds(0, size)],
                sem.scatter_s.at[0], sem.scatter_r.at[0], chip_device(other),
            ).start()

    pl.when(my_odd == 0)(lambda: scatter(0))
    pl.when(my_odd == 1)(lambda: scatter(1))
    derivatives(rank, v)
    filter_forward(rank, v)
    table_forward(rank, v)

    def reduce(odd):
        size = SMALL if odd else BIG
        v.inbox[chip, :size] = v.half[pair_rows(my_pair, odd)]
        await_bytes(v.inbox.at[pl.ds(0, CHIPS - 1), pl.ds(0, size)], sem.scatter_r.at[0])
        value = v.inbox[0, :size].astype(F32)
        for slot in range(1, CHIPS):
            value = value + v.inbox[slot, :size].astype(F32)
        rows = pair_rows(my_pair, odd, YZ * core)
        v.total[rows] = value.astype(BF16)

        for step in CHIP_STEPS:
            remote(
                v.total.at[rows], v.total.at[rows], sem.gather_s.at[0], sem.gather_r.at[0],
                chip_device(chip_at(step)),
            ).start()

    pl.when(my_odd == 0)(lambda: reduce(0))
    pl.when(my_odd == 1)(lambda: reduce(1))

    shared(v.lattice, 0)
    multiplicities(rank, v)

    def reduced(odd):
        size = SMALL if odd else BIG
        await_bytes(v.total.at[pl.ds(0, YZ - size)], sem.gather_r.at[0])
        await_bytes(v.total.at[pl.ds(0, YZ - size)], sem.scatter_s.at[0])

    pl.when(my_odd == 0)(lambda: reduced(0))
    pl.when(my_odd == 1)(lambda: reduced(1))
    swap_totals = to_mate(v.total.at[half_rows(core)], v.total.at[half_rows(core)], 1)
    swap_totals.start()
    swap_totals.wait_recv()

    coefficients(v)
    v.charge_ring[ring] = potential_pass(v).astype(BF16)
    share(v.charge_ring, 2)
    v.up[...] = upstream_table(v)
    up_rows = pl.ds(pl.multiple_of(64 * core, 64), 64)
    v.up_ring[ring] = v.up[up_rows, :]
    share(v.up_ring, 1)

    swapped_coefficients(v)
    force_pass(v)
    def added(slots):
        value = slots[0].astype(F32)
        for slot in range(1, slots.shape[0]):
            value = value + slots[slot].astype(F32)
        return value

    shared(v.charge_ring, 2)
    v.charge_mine[...] = added(v.charge_ring).astype(BF16)
    swap_charge = to_mate(v.charge_mine, v.charge_mate, 3)
    swap_charge.start()
    molecules = molecule_sums(v)
    for chunk in range(RING):
        v.message[chunk, 3:4, 0:MOLS] = molecules
        v.message[chunk, 3:4, MOLS:TILE] = jnp.zeros((1, TILE - MOLS), F32)
    for i in FAR_FIRST:
        peer = lax.rem(ring + i, RING)
        remote(v.message.at[peer], v.message_box.at[ring], sem.ring_s.at[3], sem.ring_r.at[3], ring_peer(i)).start()
    v.message_box[ring] = v.message[ring]
    swap_charge.wait_recv()
    v.charge_plane[chip] = (v.charge_mine[...].astype(F32) + v.charge_mate[...].astype(F32)).astype(BF16)
    for step in CHIP_STEPS:
        remote(
            v.charge_plane.at[chip], v.charge_plane.at[chip], sem.plane_s.at[0], sem.plane_r.at[0],
            chip_device(chip_at(step)),
        ).start()

    shared(v.up_ring, 1)
    v.up_total[up_rows, :] = added(v.up_ring).astype(BF16)
    swap_up = to_mate(v.up_total.at[up_rows], v.up_total.at[up_rows], 2)
    swap_up.start()
    swap_up.wait_recv()
    in_out[...], mid_out[...], out_out[...] = filter_backward(v)
    shared(v.message_box, 3)
    value = added(v.message_box)
    pos_out[...] = value[0:3]
    mol_out[...] = value[3:4, :MOLS]

    for swap in (swap_parts, swap_totals, swap_up, swap_charge):
        swap.wait_send()
    for phase, slots in enumerate((v.lattice, v.up_ring, v.charge_ring, v.message)):
        await_bytes(slots.at[pl.ds(0, RING - 1)], sem.ring_s.at[phase])

    def gathered(odd):
        size = SMALL if odd else BIG
        await_bytes(v.inbox.at[pl.ds(0, CHIPS - 1), pl.ds(0, size)], sem.gather_s.at[0])

    pl.when(my_odd == 0)(lambda: gathered(0))
    pl.when(my_odd == 1)(lambda: gathered(1))
    await_bytes(v.charge_plane.at[pl.ds(0, CHIPS - 1)], sem.plane_s.at[0])

    await_bytes(v.charge_plane.at[pl.ds(0, CHIPS - 1)], sem.plane_r.at[0])
    charge_out[...] = added(v.charge_plane)


def output_kernel(*refs):
    count = len(OUTS)
    sem = refs[-1]
    copies = [pltpu.make_async_copy(refs[i], refs[count + i], sem.at[i]) for i in range(count)]
    for copy in copies:
        copy.start()
    for copy in copies:
        copy.wait()


def specs(space, count):
    return [pl.BlockSpec(memory_space=space)] * count


def body(
    positions, features, charge_weight, counts, mol_ids, energy_cot,
    lattice, filter_in, filter_mid, filter_out,
):
    shape = jax.ShapeDtypeStruct
    dma = pltpu.SemaphoreType.DMA
    signs = jnp.asarray(sign_matrix(), BF16)
    signs_t = jnp.asarray(sign_matrix().T, BF16)
    outs = tuple(shape(*out) for out in OUTS)
    sums = pl.pallas_call(
        whole_kernel,
        out_shape=tuple(pltpu.VMEM(*out) for out in OUTS),
        in_specs=specs(pltpu.SMEM, 1) + specs(pl.ANY, 11),
        out_specs=tuple(specs(pltpu.VMEM, len(OUTS))),
        scratch_shapes=[pltpu.VMEM(dims, kind) for dims, kind in SCRATCH.values()]
        + [dma((count,)) for count in SEMAPHORES.values()],
        compiler_params=pltpu.CompilerParams(
            collective_id=0, has_side_effects=True, vmem_limit_bytes=56 * MIB
        ),
        name="ewald",
    )(
        counts, positions, features, charge_weight.T, mol_ids, energy_cot.reshape(1, MOLS), lattice,
        filter_in, filter_mid, filter_out.T, signs, signs_t,
    )
    mol, pos, charge, first, middle, last = pl.pallas_call(
        output_kernel,
        out_shape=outs,
        in_specs=specs(pltpu.VMEM, len(OUTS)),
        out_specs=tuple(specs(pl.ANY, len(OUTS))),
        scratch_shapes=[dma((len(OUTS),))],
        compiler_params=pltpu.CompilerParams(vmem_limit_bytes=56 * MIB),
        name="outputs",
    )(*[pltpu.with_memory_space_constraint(value, pltpu.VMEM) for value in sums])
    return (mol.reshape(MOLS), pos, charge.T, first, middle, last.T)


def solution(mesh):
    return jax.shard_map(
        body,
        mesh=mesh,
        in_specs=(
            P(None, "atoms"), P("atoms", None), P(), P("atoms"), P("atoms", None), P("atoms"),
            P(None, "kvec"), P(), P(), P(),
        ),
        out_specs=(P("atoms"), P(None, ("atoms", "kvec")), P(), P(), P(), P()),
        check_vma=False,
    )
```

```python
import functools
import math

import jax
import jax.numpy as jnp
import numpy as np
from jax import lax
from jax.experimental import pallas as pl
from jax.experimental.pallas import tpu as pltpu
from jax.sharding import PartitionSpec as P

MAXN = 12
BOX_EDGE = 40.0
MESH = pl.DeviceIdType.MESH
F32 = jnp.float32
BF16 = jnp.bfloat16

PLANE = 32
RING = 8
CAP = 4096
CH = 32
HID = 256
MOLS = 256
YZ = 640
XC = 256
HALF = 320
TILE = 512
TILES = CAP // TILE
CHIPS = 16
PAIR_ROWS = 80
BIG = 48
SMALL = 32
TABLE = 512
FAR_FIRST = (4, 3, 5, 2, 6, 1, 7)
CHIP_STEPS = sorted(
    ((dx, dy) for dx in range(4) for dy in range(4) if dx or dy),
    key=lambda step: -(min(step[0], 4 - step[0]) + min(step[1], 4 - step[1])),
)
MIB = 1 << 20


def row_of(y_index, z_index):
    if y_index is None and z_index is None:
        return 624
    if y_index is None:
        return 576 + z_index
    if z_index is None:
        return 600 + y_index
    return 24 * y_index + z_index


def half_plane():
    vectors = [(0, n3) for n3 in range(13)]
    return vectors + [(n2, n3) for n2 in range(1, 13) for n3 in range(-12, 13)]


def sign_matrix():
    def cosine(n):
        return None if n == 0 else n - 1

    def sine(n):
        return 12 + n - 1

    matrix = np.zeros((2 * HALF, YZ), np.float32)
    for index, (n2, n3) in enumerate(half_plane()):
        size, sign = abs(n3), (1.0 if n3 >= 0 else -1.0)
        matrix[index, row_of(cosine(n2), cosine(size))] = 1.0
        if n2 and size:
            matrix[index, row_of(sine(n2), sine(size))] = -sign
        if n2:
            matrix[HALF + index, row_of(sine(n2), cosine(size))] = 1.0
        if size:
            matrix[HALF + index, row_of(cosine(n2), sine(size))] = sign
    return matrix


def nt(first, second):
    return lax.dot_general(first, second, (((1,), (1,)), ((), ())), preferred_element_type=F32)


def tn(first, second):
    return lax.dot_general(first, second, (((0,), (0,)), ((), ())), preferred_element_type=F32)


def nn(first, second):
    return jnp.dot(first, second, preferred_element_type=F32)


def cos_turns(turns):
    frac = turns - jnp.floor(turns + 0.5)
    x = (2.0 * math.pi) * (0.25 - jnp.abs(frac))
    s = x * x
    poly = jnp.full_like(s, -1.0 / 39916800.0)
    for coefficient in (1.0 / 362880.0, -1.0 / 5040.0, 1.0 / 120.0, -1.0 / 6.0, 1.0):
        poly = poly * s + coefficient
    return x * poly


def rows_of_parts(value):
    high = value.astype(BF16).astype(F32)
    rest = value - high
    middle = rest.astype(BF16).astype(F32)
    low = rest - middle
    row = lax.broadcasted_iota(jnp.int32, (16, value.shape[1]), 0)
    parts = jnp.where(row == 0, high, jnp.where(row == 1, middle, jnp.where(row == 2, low, 0.0)))
    return parts.astype(BF16)


def yz_turns(coord):
    row = lax.broadcasted_iota(jnp.int32, (24, 1), 0)
    harmonic = jnp.where(row < 12, row + 1, row - 11).astype(F32)
    shift = jnp.where(row < 12, 0.0, 0.25)
    return harmonic * coord - shift, harmonic


def x_turns(coord, rank):
    row = lax.broadcasted_iota(jnp.int32, (8, 1), 0)
    harmonic = (2 * rank + lax.rem(row, 2)).astype(F32)
    shift = jnp.where(row < 2, 0.0, 0.25)
    return harmonic * coord - shift, harmonic


def lane_roll(value, shift):
    return pltpu.roll(value, shift % value.shape[1], 1)


def slope(preact, sigmoid_val):
    return sigmoid_val * (1.0 + preact * (1.0 - sigmoid_val))


def point_squares(rank, axis):
    dims = (2 * HALF, 1) if axis == 0 else (1, 2 * HALF)
    index = lax.broadcasted_iota(jnp.int32, dims, axis)
    n1 = (2 * rank + jnp.where(index >= HALF, 1, 0)).astype(F32)
    index = jnp.where(index >= HALF, index - HALF, index)
    later = (index - 13).astype(F32)
    n2 = jnp.where(index < 13, 0.0, 1.0 + jnp.floor((later + 0.5) * (1.0 / 25.0)))
    n3 = jnp.where(index < 13, index.astype(F32), later - 25.0 * (n2 - 1.0) - 12.0)
    return n1 * n1 + n2 * n2 + n3 * n3


def loop(low, high, action):
    def run(i, carry):
        action(i)
        return carry

    lax.fori_loop(low, high, run, 0)


def half_tiles(half):
    return [pl.ds(tile * TILE, TILE) for tile in range(half * TILES // 2, (half + 1) * TILES // 2)]


def functions(rank, v, half):
    for at in half_tiles(half):
        turns2, _ = yz_turns(v.pos[1:2, at])
        turns3, _ = yz_turns(v.pos[2:3, at])
        turns1, _ = x_turns(v.pos[0:1, at], rank)
        v.u2[:, at] = cos_turns(turns2)
        v.u3[:, at] = cos_turns(turns3)
        v.u1[:, at] = cos_turns(turns1)
        u3 = v.u3[:, at]
        for two in range(12):
            first = v.u2[2 * two : 2 * two + 1, at] * u3
            second = v.u2[2 * two + 1 : 2 * two + 2, at] * u3
            rows = jnp.concatenate([first, second], axis=0).astype(BF16)
            v.b[48 * two : 48 * two + 48, at] = rows
        v.b[576:624, at] = jnp.concatenate([u3, v.u2[:, at]], axis=0).astype(BF16)
        row = lax.broadcasted_iota(jnp.int32, (16, TILE), 0)
        v.b[624:640, at] = jnp.where(row == 0, 1.0, 0.0).astype(BF16)


def charges(count, v, half):
    cot_parts = rows_of_parts(v.cot[...])
    for at in half_tiles(half):
        slot = at.start + lax.broadcasted_iota(jnp.int32, (1, TILE), 1)
        alive = jnp.where(slot < count, 1.0, 0.0)
        v.alive[:, at] = alive
        molecule = lax.broadcasted_iota(jnp.int32, (MOLS, TILE), 0)
        member = jnp.where(molecule == v.ids[:, at], 1.0, 0.0).astype(BF16)
        v.member[:, at] = member
        weight = jnp.sum(nn(cot_parts, member), axis=0, keepdims=True)
        v.weight[:, at] = weight
        charge = (nt(v.cw[...], v.feat[at, :]) * alive).astype(BF16).astype(F32)
        pair = jnp.concatenate([charge, weight * charge], axis=0).astype(BF16)
        v.pair[:, at] = pair
        pair = pair.astype(F32)
        for j in range(4):
            v.a[64 * j : 64 * j + 64, at] = (v.u1[j : j + 1, at] * pair).astype(BF16)


def derivatives(rank, v):
    for half in range(2):
        for at in half_tiles(half):
            turns1, h1 = x_turns(v.pos[0:1, at], rank)
            turns2, h2 = yz_turns(v.pos[1:2, at])
            turns3, h3 = yz_turns(v.pos[2:3, at])
            v.d1[:, at] = h1 * cos_turns(turns1 + 0.25)
            v.d2[:, at] = h2 * cos_turns(turns2 + 0.25)
            v.d3[:, at] = h3 * cos_turns(turns3 + 0.25)


def structure_sum(v, rows, half):
    at = pl.ds(half * CAP // 2, CAP // 2)
    return nt(v.b[rows, at], v.a[:, at])


def network(squared, v):
    inverse = jnp.where(squared > 0.0, 1.0, 0.0) / (
        jnp.maximum(squared, 1.0) * math.sqrt(CAP * PLANE)
    )
    spacing = MAXN * math.sqrt(3.0) / 16
    center = (lax.broadcasted_iota(jnp.int32, (1, 16), 1).astype(F32) + 0.5) * spacing
    away = (jnp.sqrt(squared) - center) / spacing
    radial = jnp.exp(-0.5 * away * away).astype(BF16)
    pre_one = nn(radial, v.fin[...])
    sig_one = jax.nn.sigmoid(pre_one)
    act_one = (pre_one * sig_one).astype(BF16)
    pre_two = nn(act_one, v.fmid[...])
    sig_two = jax.nn.sigmoid(pre_two)
    act_two = (pre_two * sig_two).astype(BF16)
    logits = nn(act_two, v.fout_wide[...])
    return inverse, radial, pre_one, sig_one, act_one, pre_two, sig_two, act_two, logits


def filter_forward(rank, v):
    lane = lax.broadcasted_iota(jnp.int32, (CH, 128), 1)
    channel = lax.broadcasted_iota(jnp.int32, (CH, 128), 0)
    spread = jnp.where(lax.rem(lane, CH) == channel, 1.0, 0.0).astype(BF16)
    v.fout_wide[...] = tn(v.fout[...], spread).astype(BF16)
    values = network(point_squares(rank, 0), v)
    inverse, logits = values[0], values[-1]
    soft = jnp.maximum(logits, 0.0) + jnp.log1p(jnp.exp(-jnp.abs(logits)))
    soft = soft * inverse
    half_lane = lax.broadcasted_iota(jnp.int32, (HALF, 128), 1)
    v.filters[...] = jnp.where(half_lane < 64, soft[:HALF], soft[HALF:])


def table_forward(rank, v):
    table = lax.broadcasted_iota(jnp.int32, (TABLE, 1), 0).astype(F32)
    inverse, radial, pre_one, sig_one, act_one, pre_two, sig_two, act_two, logits = network(table, v)
    v.radial[...] = radial
    v.act_one[...] = act_one
    v.act_two[...] = act_two
    v.slope_one[...] = slope(pre_one, sig_one)
    v.slope_two[...] = slope(pre_two, sig_two)
    v.sigmoid[...] = jax.nn.sigmoid(logits) * inverse
    v.same[...] = jnp.where(table == point_squares(rank, 1), 1.0, 0.0).astype(BF16)


def multiplicities(rank, v):
    def chunk(index, total):
        k = v.lattice[index]
        k1, k2, k3 = k[0:1, :], k[1:2, :], k[2:3, :]
        back = k1 < 0
        k1 = jnp.where(back, -k1, k1)
        k2 = jnp.where(back, -k2, k2)
        k3 = jnp.where(back, -k3, k3)
        flip = (k2 < 0) | ((k2 == 0) & (k3 < 0))
        k2 = jnp.where(flip, -k2, k2)
        k3 = jnp.where(flip, -k3, k3)
        code = jnp.where(k2 == 0, k3, k2 * 25 + k3)
        width = k.shape[1]
        hit = lax.broadcasted_iota(jnp.int32, (HALF, width), 0) == code
        hit = jnp.where(hit, 1.0, 0.0).astype(BF16)
        row = lax.broadcasted_iota(jnp.int32, (16, width), 0)
        own = (k1 - 2 * rank) == lax.rem(row, 2)
        sign = jnp.where((row >= 2) & flip, -1.0, 1.0)
        select = jnp.where(own & (row < 4), sign, 0.0).astype(BF16)
        return total + nt(hit, select)

    counted = lax.fori_loop(0, RING, chunk, jnp.zeros((HALF, 16), F32))
    lane = lax.broadcasted_iota(jnp.int32, (HALF, 128), 1)
    v.both[...] = jnp.where(lane < 64, counted[:, 0:1], counted[:, 1:2])
    v.difference[...] = jnp.where(lane < 64, counted[:, 2:3], counted[:, 3:4])
    v.filter_both[...] = v.filters[...] * v.both[...]
    v.filter_difference[...] = v.filters[...] * v.difference[...]


def coefficients(v):
    signs = v.signs[...]
    total = jnp.concatenate(
        [
            jnp.concatenate([v.total[start : start + HALF], v.total[start + HALF : start + YZ]], axis=1)
            for start in (0, YZ)
        ],
        axis=0,
    )
    v.sums[...] = nn(signs, total)
    ncc, ncs = v.sums[:HALF, :128], v.sums[HALF:, :128]
    nsc, nss = v.sums[:HALF, 128:], v.sums[HALF:, 128:]
    fp, fd = v.filter_both[...], v.filter_difference[...]
    gcc = (fp * ncc - fd * nss).astype(BF16)
    gss = (fp * nss - fd * ncc).astype(BF16)
    gsc = (fp * nsc + fd * ncs).astype(BF16)
    gcs = (fp * ncs + fd * nsc).astype(BF16)
    v.coef[:HALF, :128] = gcc
    v.coef[HALF:, :128] = gcs
    v.coef[:HALF, 128:] = gsc
    v.coef[HALF:, 128:] = gss
    v.gt[...] = tn(v.coef[...], signs).astype(BF16)


def swapped_coefficients(v):
    g = nn(v.signs_t[...], v.coef[...])
    lane = lax.broadcasted_iota(jnp.int32, (YZ, XC), 1)
    swapped = jnp.where(lax.rem(lane, 64) < 32, lane_roll(g, -32), lane_roll(g, 32))
    v.gs[...] = swapped.astype(BF16)


def upstream_table(v):
    ncc, ncs = v.sums[:HALF, :128], v.sums[HALF:, :128]
    nsc, nss = v.sums[:HALF, 128:], v.sums[HALF:, 128:]
    tcc, tcs = lane_roll(ncc, -32), lane_roll(ncs, -32)
    tsc, tss = lane_roll(nsc, -32), lane_roll(nss, -32)
    upstream = 0.5 * (
        v.both[...] * (ncc * tcc + nss * tss + nsc * tsc + ncs * tcs)
        + v.difference[...] * (nsc * tcs + ncs * tsc - ncc * tss - nss * tcc)
    )
    upstream = jnp.concatenate([upstream, lane_roll(upstream, -64)], axis=0)
    lane = lax.broadcasted_iota(jnp.int32, (2 * HALF, 128), 1)
    upstream = jnp.where(lane < CH, upstream, 0.0)
    total = nn(v.same[0:128, :], upstream.astype(BF16))
    for group in range(1, 4):
        rows = v.same[128 * group : 128 * group + 128, :]
        total = total + nn(rows, lane_roll(upstream, 32 * group).astype(BF16))
    return total.astype(BF16)


def filter_backward(v):
    upstream = v.up_total[...].astype(F32)
    upstream = jnp.concatenate(
        [upstream] + [lane_roll(upstream, -32 * group) for group in range(1, 4)], axis=0
    )
    lane = lax.broadcasted_iota(jnp.int32, (TABLE, 128), 1)
    grad_logits = jnp.where(lane < CH, upstream * v.sigmoid[...], 0.0).astype(BF16)
    out_grad = tn(grad_logits, v.act_two[...])
    grad_two = (nt(grad_logits, v.fout_wide[...]) * v.slope_two[...]).astype(BF16)
    mid_grad = tn(v.act_one[...], grad_two)
    grad_one = (nt(grad_two, v.fmid[...]) * v.slope_one[...]).astype(BF16)
    return tn(v.radial[...], grad_one), mid_grad, out_grad[:CH]


GRAD_SCALE = 0.5 * 2.0 * math.pi / BOX_EDGE


def potential_pass(v):
    for tile in range(TILES):
        at = pl.ds(tile * TILE, TILE)
        u1 = v.u1[:, at]
        w = nn(v.gt[...], v.b[:, at])
        v.w[:, at] = w
        pot = sum(u1[j : j + 1, :] * w[64 * j : 64 * j + 64, :] for j in range(4))
        volt, other = pot[:CH], pot[CH:]
        v.volt[:, at] = volt
        v.cot_rows[:, at] = (0.5 * (v.weight[:, at] * volt + other) * v.alive[:, at]).astype(BF16)
    return nn(v.cot_rows[...], v.feat[...])


def molecule_sums(v):
    return jnp.sum(nt(rows_of_parts(v.energy[...]), v.member[...]), axis=0, keepdims=True)


def force_pass(v):
    def fold(value):
        return value[0:8] + value[8:16] + value[16:24]

    for tile in range(TILES):
        at = pl.ds(tile * TILE, TILE)
        v.response[:, at] = nn(v.gs[...], v.a[:, at])
        pair = v.pair[:, at].astype(F32)
        charge, weighted = pair[:CH], pair[CH:]
        v.energy[:, at] = 0.5 * jnp.sum(charge * v.volt[:, at], axis=0, keepdims=True)
        potx = sum(v.d1[j : j + 1, at] * v.w[64 * j : 64 * j + 64, at] for j in range(4))
        grad_x = jnp.sum(weighted * potx[:CH] + charge * potx[CH:], axis=0, keepdims=True)
        u3, d3 = v.u3[:, at], v.d3[:, at]
        sum_y = fold(v.d2[:, at] * v.response[600:624, at])
        sum_z = fold(d3 * v.response[576:600, at])
        for y in range(24):
            response = v.response[24 * y : 24 * y + 24, at]
            sum_y = sum_y + v.d2[y : y + 1, at] * fold(u3 * response)
            sum_z = sum_z + v.u2[y : y + 1, at] * fold(d3 * response)
        v.message[tile, 0:1, :] = grad_x * GRAD_SCALE
        v.message[tile, 1:2, :] = jnp.sum(sum_y, axis=0, keepdims=True) * GRAD_SCALE
        v.message[tile, 2:3, :] = jnp.sum(sum_z, axis=0, keepdims=True) * GRAD_SCALE


SCRATCH = dict(
    pos=((3, CAP), F32), feat=((CAP, 128), BF16), cw=((CH, 128), BF16), ids=((1, CAP), jnp.int32),
    cot=((1, MOLS), F32), fin=((16, HID), BF16), fmid=((HID, HID), BF16), fout=((CH, HID), BF16),
    signs=((2 * HALF, YZ), BF16), signs_t=((YZ, 2 * HALF), BF16), lattice=((RING, 3, 1024), jnp.int32),
    u1=((8, CAP), F32), u2=((24, CAP), F32), u3=((24, CAP), F32), d1=((8, CAP), F32), d2=((24, CAP), F32), d3=((24, CAP), F32),
    w=((XC, CAP), F32), volt=((CH, CAP), F32),
    alive=((1, CAP), F32), weight=((1, CAP), F32), member=((MOLS, CAP), BF16),
    pair=((2 * CH, CAP), BF16), b=((YZ, CAP), BF16), a=((XC, CAP), BF16), acc=((YZ, XC), F32),
    part=((YZ, 128), BF16), mate=((YZ, 128), BF16), half=((YZ, 128), BF16),
    inbox=((CHIPS, BIG, 128), BF16), total=((2 * YZ, 128), BF16),
    radial=((TABLE, 16), BF16), act_one=((TABLE, HID), BF16), act_two=((TABLE, HID), BF16),
    slope_one=((TABLE, HID), F32), slope_two=((TABLE, HID), F32), fout_wide=((HID, 128), BF16),
    sigmoid=((TABLE, 128), F32), same=((TABLE, 2 * HALF), BF16), filters=((HALF, 128), F32),
    both=((HALF, 128), F32), difference=((HALF, 128), F32),
    filter_both=((HALF, 128), F32), filter_difference=((HALF, 128), F32),
    sums=((2 * HALF, XC), F32), coef=((2 * HALF, XC), BF16), energy=((1, CAP), F32), cot_rows=((CH, CAP), BF16),
    gt=((XC, YZ), BF16), gs=((YZ, XC), BF16), response=((YZ, CAP), F32),
    up=((128, 128), BF16), up_ring=((RING, 64, 128), BF16), up_total=((128, 128), BF16),
    message=((RING, 4, TILE), F32), message_box=((RING, 4, TILE), F32),
    charge_ring=((RING, CH, 128), BF16), charge_mine=((CH, 128), BF16), charge_mate=((CH, 128), BF16),
    charge_plane=((CHIPS, CH, 128), BF16),
)
SEMAPHORES = dict(
    load=11, mate_s=4, mate_r=4, scatter_s=1, scatter_r=1, gather_s=1, gather_r=1,
    ring_s=4, ring_r=4, plane_s=1, plane_r=1,
)
OUTS = (
    ((1, MOLS), F32), ((3, TILE), F32), ((CH, 128), F32), ((16, HID), F32), ((HID, HID), F32), ((CH, HID), F32),
)


class Names:
    def __init__(self, names, refs):
        for name, ref in zip(names, refs, strict=True):
            setattr(self, name, ref)


def whole_kernel(
    count_ref, pos_ref, feat_ref, cw_ref, ids_ref, cot_ref, lattice_ref, fin_ref, fmid_ref, fout_ref,
    signs_ref, signs_t_ref, mol_out, pos_out, charge_out, in_out, mid_out, out_out, *scratch,
):
    v = Names(SCRATCH, scratch[: len(SCRATCH)])
    sem = Names(SEMAPHORES, scratch[len(SCRATCH) :])
    plane, ring = lax.axis_index("atoms"), lax.axis_index("kvec")
    chip, core = plane // 2, lax.rem(plane, 2)
    rank = ring

    loads = [
        pltpu.make_async_copy(src, dst, sem.load.at[i])
        for i, (src, dst) in enumerate((
            (pos_ref, v.pos), (feat_ref, v.feat), (cw_ref, v.cw), (ids_ref, v.ids), (cot_ref, v.cot),
            (lattice_ref, v.lattice.at[ring]), (fin_ref, v.fin), (fmid_ref, v.fmid), (fout_ref, v.fout),
            (signs_ref, v.signs), (signs_t_ref, v.signs_t),
        ))
    ]
    for load in loads:
        load.start()
    def remote(src, dst, send, recv, device):
        return pltpu.make_async_remote_copy(
            src_ref=src, dst_ref=dst, send_sem=send, recv_sem=recv,
            device_id=device, device_id_type=MESH,
        )

    def await_bytes(ref, semaphore):
        pltpu.make_async_copy(ref, ref, semaphore).wait()

    def ring_peer(i):
        return (plane, lax.rem(ring + i, RING))

    def chip_device(which):
        return (2 * which + core, ring)

    def chip_at(step):
        return 4 * lax.rem(chip // 4 + step[0], 4) + lax.rem(lax.rem(chip, 4) + step[1], 4)

    mate = (plane + 1 - 2 * core, ring)

    barrier = pltpu.get_barrier_semaphore()

    def greet(device):
        pl.semaphore_signal(barrier, inc=1, device_id=device, device_id_type=MESH)

    loop(1, CHIPS, lambda i: greet(chip_device(lax.rem(chip + i, CHIPS))))
    loop(1, RING, lambda i: greet(ring_peer(i)))
    greet(mate)

    loads[0].wait()
    functions(rank, v, 0)
    for load in loads[1:5]:
        load.wait()
    charges(count_ref[0], v, 0)
    v.acc[...] = structure_sum(v, pl.ds(0, YZ), 0)
    functions(rank, v, 1)
    charges(count_ref[0], v, 1)

    def share(slots, phase):
        for i in FAR_FIRST:
            remote(slots.at[ring], slots.at[ring], sem.ring_s.at[phase], sem.ring_r.at[phase], ring_peer(i)).start()

    def shared(slots, phase):
        await_bytes(slots.at[pl.ds(0, RING - 1)], sem.ring_r.at[phase])

    def half_rows(which):
        return pl.ds(pl.multiple_of(YZ * which, YZ), YZ)

    def to_mate(src, dst, phase):
        return remote(src, dst, sem.mate_s.at[phase], sem.mate_r.at[phase], mate)

    def row_sums(which):
        rows = pl.ds(pl.multiple_of(HALF * which, HALF), HALF)
        return v.acc[rows, :] + structure_sum(v, rows, 1)

    theirs = row_sums(1 - core)
    v.part[:HALF, :] = theirs[:, :128].astype(BF16)
    v.part[HALF:, :] = theirs[:, 128:].astype(BF16)
    pl.semaphore_wait(barrier, CHIPS + RING - 1)
    swap_parts = to_mate(v.part, v.mate, 0)
    swap_parts.start()
    for load in loads[5:]:
        load.wait()
    share(v.lattice, 0)
    mine = row_sums(core)
    swap_parts.wait_recv()
    v.half[:HALF, :] = (mine[:, :128] + v.mate[:HALF, :].astype(F32)).astype(BF16)
    v.half[HALF:, :] = (mine[:, 128:] + v.mate[HALF:, :].astype(F32)).astype(BF16)

    def pair_rows(which, odd, base=0):
        start = base + PAIR_ROWS * which + (BIG if odd else 0)
        return pl.ds(pl.multiple_of(start, 16), SMALL if odd else BIG)

    my_pair, my_odd = chip // 2, lax.rem(chip, 2)

    def scatter(odd):
        for step in CHIP_STEPS:
            other = chip_at(step)
            other_odd = (odd + step[1]) % 2
            size = SMALL if other_odd else BIG
            remote(
                v.half.at[pair_rows(other // 2, other_odd)], v.inbox.at[chip, pl.ds(0, size)],
                sem.scatter_s.at[0], sem.scatter_r.at[0], chip_device(other),
            ).start()

    pl.when(my_odd == 0)(lambda: scatter(0))
    pl.when(my_odd == 1)(lambda: scatter(1))
    derivatives(rank, v)
    filter_forward(rank, v)
    table_forward(rank, v)

    def reduce(odd):
        size = SMALL if odd else BIG
        v.inbox[chip, :size] = v.half[pair_rows(my_pair, odd)]
        await_bytes(v.inbox.at[pl.ds(0, CHIPS - 1), pl.ds(0, size)], sem.scatter_r.at[0])
        value = v.inbox[0, :size].astype(F32)
        for slot in range(1, CHIPS):
            value = value + v.inbox[slot, :size].astype(F32)
        rows = pair_rows(my_pair, odd, YZ * core)
        v.total[rows] = value.astype(BF16)

        for step in CHIP_STEPS:
            remote(
                v.total.at[rows], v.total.at[rows], sem.gather_s.at[0], sem.gather_r.at[0],
                chip_device(chip_at(step)),
            ).start()

    pl.when(my_odd == 0)(lambda: reduce(0))
    pl.when(my_odd == 1)(lambda: reduce(1))

    shared(v.lattice, 0)
    multiplicities(rank, v)

    def reduced(odd):
        size = SMALL if odd else BIG
        await_bytes(v.total.at[pl.ds(0, YZ - size)], sem.gather_r.at[0])
        await_bytes(v.total.at[pl.ds(0, YZ - size)], sem.scatter_s.at[0])

    pl.when(my_odd == 0)(lambda: reduced(0))
    pl.when(my_odd == 1)(lambda: reduced(1))
    swap_totals = to_mate(v.total.at[half_rows(core)], v.total.at[half_rows(core)], 1)
    swap_totals.start()
    swap_totals.wait_recv()

    coefficients(v)
    v.charge_ring[ring] = potential_pass(v).astype(BF16)
    share(v.charge_ring, 2)
    v.up[...] = upstream_table(v)
    up_rows = pl.ds(pl.multiple_of(64 * core, 64), 64)
    v.up_ring[ring] = v.up[up_rows, :]
    share(v.up_ring, 1)

    swapped_coefficients(v)
    force_pass(v)
    molecules = molecule_sums(v)
    for chunk in range(RING):
        v.message[chunk, 3:4, 0:MOLS] = molecules
        v.message[chunk, 3:4, MOLS:TILE] = jnp.zeros((1, TILE - MOLS), F32)
    for i in FAR_FIRST:
        peer = lax.rem(ring + i, RING)
        remote(v.message.at[peer], v.message_box.at[ring], sem.ring_s.at[3], sem.ring_r.at[3], ring_peer(i)).start()
    v.message_box[ring] = v.message[ring]

    def added(slots):
        value = slots[0].astype(F32)
        for slot in range(1, slots.shape[0]):
            value = value + slots[slot].astype(F32)
        return value

    shared(v.charge_ring, 2)
    v.charge_mine[...] = added(v.charge_ring).astype(BF16)
    swap_charge = to_mate(v.charge_mine, v.charge_mate, 3)
    swap_charge.start()
    swap_charge.wait_recv()
    v.charge_plane[chip] = (v.charge_mine[...].astype(F32) + v.charge_mate[...].astype(F32)).astype(BF16)
    for step in CHIP_STEPS:
        remote(
            v.charge_plane.at[chip], v.charge_plane.at[chip], sem.plane_s.at[0], sem.plane_r.at[0],
            chip_device(chip_at(step)),
        ).start()

    shared(v.up_ring, 1)
    v.up_total[up_rows, :] = added(v.up_ring).astype(BF16)
    swap_up = to_mate(v.up_total.at[up_rows], v.up_total.at[up_rows], 2)
    swap_up.start()
    swap_up.wait_recv()
    in_out[...], mid_out[...], out_out[...] = filter_backward(v)
    shared(v.message_box, 3)
    value = added(v.message_box)
    pos_out[...] = value[0:3]
    mol_out[...] = value[3:4, :MOLS]

    for swap in (swap_parts, swap_totals, swap_up, swap_charge):
        swap.wait_send()
    for phase, slots in enumerate((v.lattice, v.up_ring, v.charge_ring, v.message)):
        await_bytes(slots.at[pl.ds(0, RING - 1)], sem.ring_s.at[phase])

    def gathered(odd):
        size = SMALL if odd else BIG
        await_bytes(v.inbox.at[pl.ds(0, CHIPS - 1), pl.ds(0, size)], sem.gather_s.at[0])

    pl.when(my_odd == 0)(lambda: gathered(0))
    pl.when(my_odd == 1)(lambda: gathered(1))
    await_bytes(v.charge_plane.at[pl.ds(0, CHIPS - 1)], sem.plane_s.at[0])

    await_bytes(v.charge_plane.at[pl.ds(0, CHIPS - 1)], sem.plane_r.at[0])
    charge_out[...] = added(v.charge_plane)


def output_kernel(*refs):
    count = len(OUTS)
    sem = refs[-1]
    copies = [pltpu.make_async_copy(refs[i], refs[count + i], sem.at[i]) for i in range(count)]
    for copy in copies:
        copy.start()
    for copy in copies:
        copy.wait()


def specs(space, count):
    return [pl.BlockSpec(memory_space=space)] * count


def body(
    positions, features, charge_weight, counts, mol_ids, energy_cot,
    lattice, filter_in, filter_mid, filter_out,
):
    shape = jax.ShapeDtypeStruct
    dma = pltpu.SemaphoreType.DMA
    signs = jnp.asarray(sign_matrix(), BF16)
    signs_t = jnp.asarray(sign_matrix().T, BF16)
    outs = tuple(shape(*out) for out in OUTS)
    sums = pl.pallas_call(
        whole_kernel,
        out_shape=tuple(pltpu.VMEM(*out) for out in OUTS),
        in_specs=specs(pltpu.SMEM, 1) + specs(pl.ANY, 11),
        out_specs=tuple(specs(pltpu.VMEM, len(OUTS))),
        scratch_shapes=[pltpu.VMEM(dims, kind) for dims, kind in SCRATCH.values()]
        + [dma((count,)) for count in SEMAPHORES.values()],
        compiler_params=pltpu.CompilerParams(
            collective_id=0, has_side_effects=True, vmem_limit_bytes=56 * MIB
        ),
        name="ewald",
    )(
        counts, positions, features, charge_weight.T, mol_ids, energy_cot.reshape(1, MOLS), lattice,
        filter_in, filter_mid, filter_out.T, signs, signs_t,
    )
    mol, pos, charge, first, middle, last = pl.pallas_call(
        output_kernel,
        out_shape=outs,
        in_specs=specs(pltpu.VMEM, len(OUTS)),
        out_specs=tuple(specs(pl.ANY, len(OUTS))),
        scratch_shapes=[dma((len(OUTS),))],
        compiler_params=pltpu.CompilerParams(vmem_limit_bytes=56 * MIB),
        name="outputs",
    )(*[pltpu.with_memory_space_constraint(value, pltpu.VMEM) for value in sums])
    return (mol.reshape(MOLS), pos, charge.T, first, middle, last.T)


def solution(mesh):
    return jax.shard_map(
        body,
        mesh=mesh,
        in_specs=(
            P(None, "atoms"), P("atoms", None), P(), P("atoms"), P("atoms", None), P("atoms"),
            P(None, "kvec"), P(), P(), P(),
        ),
        out_specs=(P("atoms"), P(None, ("atoms", "kvec")), P(), P(), P(), P()),
        check_vma=False,
    )
```
